32 devices in a mesh: blk: 16 (over z, y, core), frq: 2 (over x).
Axes of the slice: x: 2, y: 2, z: 4, core: 2. Of those that a mesh axis runs over, the one named last changes fastest.
Arguments:
- spectra: bfloat16 [2, 4096, 4, 2048], P(None, 'blk', None, 'frq'), may hold values from -6 to 6
- channel_valid: int32 [4096], P('blk'), may hold values 0 or 1
Outputs:
- stacked: float32 [16, 4, 201, 256], P('blk', None, None, 'frq')
The draws below stay inside these ranges and needn't reach their ends.
Inputs may be any that keep to these rules, and one draw needn't show every extreme that they name: `channel_valid`: 1 marks a usable channel.
All inputs are finite; a program needn't handle non-finite values. No bound on the sum of `channel_valid` on one device may be relied on, other than what follows from the above.
Results may differ from the reference program's by a relative error of at most 0.006.
Values may be sent and summed in bfloat16 or wider, within the bound.
No kernel may reach another device: no remote copies, remote signals or barrier semaphores. Data moves between devices by JAX's collectives and lax.ppermute only.
A program may use at most 384 MiB of HBM per device.

```python
import math
import jax
import jax.numpy as jnp
from jax import lax

CB = 256
W = 4
F = 2048
LAGS = 201
ROUNDS = 4
CH = 4096
N_BLK = 16


def with_ends(array, key, smallest, top_value):
    place = [jax.random.randint(jax.random.fold_in(key, axis), (), 0, length) for axis, length in enumerate(array.shape)]
    main_axis = array.shape.index(max(array.shape))
    beside = place[:main_axis] + [(place[main_axis] + 1) % array.shape[main_axis]] + place[main_axis + 1:]
    return array.at[tuple(place)].set(smallest).at[tuple(beside)].set(top_value)


def shard_levels(key, shape, split, smallest, top_value):
    level, own = 1.0, jax.random.fold_in(key, 6)
    for dim, blocks in split:
        heights = jnp.exp(jax.random.uniform(jax.random.fold_in(own, dim), (blocks,), jnp.float32, smallest / len(split), top_value / len(split)))
        level = level * jnp.repeat(heights, shape[dim] // blocks).reshape([-1 if axis == dim else 1 for axis in range(len(shape))])
    return level


def noise(key, extent, deviation, reach, split=(), held_as=jnp.bfloat16):
    gain = shard_levels(key, extent, split, -0.22, 0.18) if split else 1.0
    result = jax.random.normal(key, extent, jnp.float32) * deviation * gain
    return jnp.minimum(jnp.maximum(result, -reach), reach).astype(held_as)


def setup_inputs(seed: int = 0) -> dict:
    key_of = jax.random.split(jax.random.key(seed), 3)
    spectra = noise(key_of[0], (2, CH, W, F), 1.0, 6.0, ((1, 16), (3, 2)))
    channel_valid = with_ends((jax.random.randint(key_of[1], (CH,), 0, 8) < 7).astype(jnp.int32), jax.random.fold_in(key_of[1], 1), 0, 1)
    return {"spectra": spectra, "channel_valid": channel_valid}


def matmul_high(left, right):
    return jnp.dot(left, right, precision=lax.Precision.HIGHEST, preferred_element_type=jnp.float32)

def angle_table(first_index, second_index, period):
    product = jnp.mod(first_index[:, None] * second_index[None, :], period)
    return 2.0 * math.pi / period * product.astype(jnp.float32)

def split_table(table):
    upper = table.astype(jnp.bfloat16)
    lower = (table - upper.astype(jnp.float32)).astype(jnp.bfloat16)
    return (upper, lower)

def twiddle_product(pair, data):
    return jnp.dot(pair[0], data, preferred_element_type=jnp.float32) + jnp.dot(pair[1], data, preferred_element_type=jnp.float32)

def to_wavenumber(spectrum_in, cos_pair, sin_pair):
    channels = spectrum_in.shape[1]
    flattened = spectrum_in.reshape(2, channels, -1)
    real_part = twiddle_product(cos_pair, flattened[0]) + twiddle_product(sin_pair, flattened[1])
    imag_part = twiddle_product(cos_pair, flattened[1]) - twiddle_product(sin_pair, flattened[0])
    return jnp.stack([real_part, imag_part])

def lag_terms(own_hat, far_hat, windows, inv_cos, inv_sin, lag_cos, lag_sin, normalizer):
    length = own_hat.shape[1]
    own_hat = own_hat.reshape(2, length, windows, -1)
    far_hat = far_hat.reshape(2, length, windows, -1)
    cross_real = lax.optimization_barrier(jnp.sum(own_hat[0] * far_hat[0] + own_hat[1] * far_hat[1], axis=1))
    cross_imag = lax.optimization_barrier(jnp.sum(own_hat[1] * far_hat[0] - own_hat[0] * far_hat[1], axis=1))
    stack_real = matmul_high(inv_cos, cross_real) - matmul_high(inv_sin, cross_imag)
    stack_imag = matmul_high(inv_sin, cross_real) + matmul_high(inv_cos, cross_imag)
    return normalizer * (matmul_high(lag_cos, stack_real.T) - matmul_high(lag_sin, stack_imag.T))

def reference(spectra, channel_valid):
    spectra_f = spectra.astype(jnp.float32)
    mean_power = lax.optimization_barrier(jnp.mean(spectra_f[0] * spectra_f[0] + spectra_f[1] * spectra_f[1], axis=1, keepdims=True))
    whiten_scale = channel_valid.astype(jnp.float32)[:, None, None] / jnp.maximum(jnp.sqrt(mean_power), 0.5)
    whitened = (spectra_f * whiten_scale[None]).astype(jnp.bfloat16)
    blocks = jnp.moveaxis(whitened.reshape(2, N_BLK, CB, W, F), 1, 0)
    length = 2 * CB
    chan_index = jnp.arange(CB, dtype=jnp.int32)
    wave_index = jnp.arange(length, dtype=jnp.int32)
    fwd_angle = angle_table(wave_index, chan_index, length)
    cos_pair = split_table(jnp.cos(fwd_angle))
    sin_pair = split_table(jnp.sin(fwd_angle))
    inv_angle = angle_table(chan_index - CB // 2, wave_index, length)
    inv_cos, inv_sin = (jnp.cos(inv_angle) / length, jnp.sin(inv_angle) / length)
    lag_index = jnp.arange(LAGS, dtype=jnp.int32) - (LAGS - 1) // 2
    freq_index = jnp.arange(F, dtype=jnp.int32)
    lag_angle = angle_table(lag_index, freq_index, 2 * F)
    lag_cos, lag_sin = (jnp.cos(lag_angle), jnp.sin(lag_angle))
    normalizer = 1.0 / math.sqrt(W * CB * F)

    def scan_block(history, block):
        own_hat = to_wavenumber(block, cos_pair, sin_pair)
        results = [lag_terms(own_hat, history[index], W, inv_cos, inv_sin, lag_cos, lag_sin, normalizer) for index in range(ROUNDS)]
        history = jnp.concatenate([own_hat[None], history[:-1]], axis=0)
        return (history, jnp.stack(results))
    start_history = jnp.zeros((ROUNDS, 2, length, W * F), jnp.float32)
    final_history, stacked = lax.scan(scan_block, start_history, blocks)
    return stacked
```

```python
import functools
import math

import jax
import jax.numpy as jnp
import ml_dtypes
import numpy as np
from jax import lax
from jax.experimental import pallas as pl
from jax.experimental.pallas import tpu as pltpu
from jax.sharding import PartitionSpec as P

LAGS = 201
ROUNDS = 4
GROUP = 4
PARTS = 2
LANES = 128
F32, BF16 = jnp.float32, jnp.bfloat16


def after(value, *others):
    return lax.optimization_barrier((value, others))[0]


def pair_list(part):
    pairs = []
    for own in range(GROUP):
        for distance in range(1, ROUNDS + 1):
            far = own - distance
            if far >= 0:
                pairs.append((own, far))
            elif part == 0:
                pairs.append((GROUP + own, far + GROUP))
            else:
                pairs.append((own, GROUP + far + GROUP))
    return pairs


def whiten_kernel(pieces, items, pos_ref, valid_ref, *refs):
    ins, outs, held = refs[: len(pieces)], refs[len(pieces) : -1], refs[-1]
    tile, windows = ins[0].shape[1:3]
    place = (tile, valid_ref.shape[1])
    row = lax.broadcasted_iota(jnp.int32, place, 0) + pl.program_id(0) * tile
    here = row == lax.broadcasted_iota(jnp.int32, place, 1)
    valid = jnp.sum(jnp.where(here, valid_ref[...].astype(F32), 0.0), axis=1, keepdims=True)
    for at, piece in enumerate(pieces):
        for half in range(2):
            held[at, half] = ins[at][half].reshape(tile * windows, LANES).astype(F32)
        values = [
            [held[at, half, pl.ds(w, tile, stride=windows), :] for half in range(2)] for w in range(windows)
        ]
        power = values[0][0] * values[0][0] + values[0][1] * values[0][1]
        for real, imag in values[1:]:
            power = power + (real * real + imag * imag)
        scale = valid / jnp.maximum(jnp.sqrt(power * (1.0 / windows)), 0.5)
        for w in range(windows):
            both = jnp.concatenate([values[w][half] * scale for half in range(2)], axis=1).astype(BF16)
            for item, out in zip(items, outs):
                for index, wanted in enumerate(item):
                    if wanted == piece:
                        out[index, w] = both


def whiten(spectra, valid, pos, items):
    _, channels, windows, freqs = spectra.shape
    parts = freqs // (GROUP * LANES)
    tile = min(64, channels)
    pieces = sorted({piece for item in items for piece in item})
    in_specs = [pl.BlockSpec((1, channels), lambda i, pos: (0, 0))] + [
        pl.BlockSpec(
            (2, tile, windows, LANES),
            lambda i, pos, flip=flip, part=part: (0, i, 0, (pos[0] ^ flip) * parts + part),
        )
        for flip, part in pieces
    ]
    out_specs = [pl.BlockSpec((len(item), windows, tile, 2 * LANES), lambda i, pos: (0, 0, i, 0)) for item in items]
    return pl.pallas_call(
        functools.partial(whiten_kernel, pieces, items),
        grid_spec=pltpu.PrefetchScalarGridSpec(
            num_scalar_prefetch=1,
            grid=(channels // tile,),
            in_specs=in_specs,
            out_specs=out_specs,
            scratch_shapes=[pltpu.VMEM((len(pieces), 2, tile * windows, LANES), F32)],
        ),
        out_shape=[jax.ShapeDtypeStruct((len(item), windows, channels, 2 * LANES), BF16) for item in items],
        compiler_params=pltpu.CompilerParams(vmem_limit_bytes=56 << 20),
        cost_estimate=pl.CostEstimate(flops=0, bytes_accessed=1000, transcendentals=0),
        name="whiten",
    )(pos, valid, *([spectra] * len(pieces)))


def correlate_kernel(pairs, pos_ref, *refs):
    blocks = refs[: 2 * GROUP]
    fwd_ref, lag_ref, inv_ref, keep_ref, send_ref, hat, plus, cross = refs[2 * GROUP :]
    w = pl.program_id(0)
    windows = pl.num_programs(0)
    member = pos_ref[0]
    half = fwd_ref.shape[0] // 2
    for index in range(2 * GROUP):
        slot = (member ^ (index % GROUP)) + (index // GROUP) * GROUP
        terms = jnp.dot(fwd_ref[...], blocks[index][0, 0], preferred_element_type=F32)
        cos_r, cos_i = terms[:half, :LANES], terms[:half, LANES:]
        sin_r, sin_i = terms[half:, :LANES], terms[half:, LANES:]
        hat[slot, w, 0] = cos_r + sin_i
        hat[slot, w, 1] = cos_i - sin_r
        hat[slot, w, 2] = cos_r - sin_i
        hat[slot, w, 3] = cos_i + sin_r

    @pl.when(w == windows - 1)
    def _():
        def products(step, carry):
            rows = pl.ds(pl.multiple_of(step * 8, 8), 8)
            odd_rows = pl.ds(pl.multiple_of(half + step * 8, 8), 8)
            sums = []
            for sign in range(2):
                sums = [None] * (2 * len(pairs))
                for win in range(hat.shape[1]):
                    real = [hat[slot, win, 2 * sign, rows, :] for slot in range(2 * GROUP)]
                    imag = [hat[slot, win, 2 * sign + 1, rows, :] for slot in range(2 * GROUP)]
                    for n, (own, far) in enumerate(pairs):
                        part_r = real[own] * real[far] + imag[own] * imag[far]
                        part_i = imag[own] * real[far] - real[own] * imag[far]
                        sums[2 * n] = part_r if win == 0 else sums[2 * n] + part_r
                        sums[2 * n + 1] = part_i if win == 0 else sums[2 * n + 1] + part_i
                for n in range(len(pairs)):
                    if sign == 0:
                        plus[2 * n], plus[2 * n + 1] = sums[2 * n], sums[2 * n + 1]
                    else:
                        plus_r, plus_i = plus[2 * n], plus[2 * n + 1]
                        minus_r, minus_i = sums[2 * n], sums[2 * n + 1]
                        cross[n, rows, :LANES] = plus_r + minus_r
                        cross[n, rows, LANES:] = plus_i + minus_i
                        cross[n, odd_rows, :LANES] = plus_i - minus_i
                        cross[n, odd_rows, LANES:] = minus_r - plus_r
            return carry

        lax.fori_loop(0, half // 8, products, 0)

        def lags(n, carry):
            folded = cross[n].astype(BF16)
            by_offset = jnp.dot(inv_ref[...], folded, preferred_element_type=F32).astype(BF16)
            result = jnp.dot(by_offset, lag_ref[0], preferred_element_type=F32).astype(BF16)
            flip = (n // ROUNDS) ^ member
            place, distance = flip // 2, n % ROUNDS

            @pl.when(flip % 2 == 0)
            def _():
                keep_ref[place, distance] = result

            @pl.when(flip % 2 == 1)
            def _():
                send_ref[place, distance] = result

            return carry

        lax.fori_loop(0, len(pairs), lags, 0, unroll=4)


def correlate(pos, part, blocks, tables):
    fwd, lag, inv = tables
    _, windows, channels, lanes = blocks[0][0].shape
    width = lag.shape[2]
    pairs = pair_list(part)
    half = fwd.shape[0] // 2
    in_specs = [
        pl.BlockSpec((1, 1, channels, lanes), lambda w, pos, place=place: (place, w, 0, 0)) for _, place in blocks
    ] + [
        pl.BlockSpec(fwd.shape, lambda w, pos: (0, 0)),
        pl.BlockSpec((1, lanes, width), lambda w, pos: ((pos[1] * GROUP + pos[0]) * PARTS + part, 0, 0)),
        pl.BlockSpec(inv.shape, lambda w, pos: (0, 0)),
    ]
    out_spec = pl.BlockSpec((2, ROUNDS, channels, width), lambda w, pos: (0, 0, 0, 0))
    return pl.pallas_call(
        functools.partial(correlate_kernel, pairs),
        grid_spec=pltpu.PrefetchScalarGridSpec(
            num_scalar_prefetch=1,
            grid=(windows,),
            in_specs=in_specs,
            out_specs=[out_spec, out_spec],
            scratch_shapes=[
                pltpu.VMEM((2 * GROUP, windows, 4, half, LANES), F32),
                pltpu.VMEM((2 * len(pairs), 8, LANES), F32),
                pltpu.VMEM((len(pairs), 2 * half, 2 * LANES), F32),
            ],
        ),
        out_shape=[jax.ShapeDtypeStruct((2, ROUNDS, channels, width), BF16)] * 2,
        compiler_params=pltpu.CompilerParams(vmem_limit_bytes=48 << 20),
        cost_estimate=pl.CostEstimate(flops=0, bytes_accessed=1000, transcendentals=0),
        name="correlate",
    )(pos, *[array for array, _ in blocks], fwd, lag, inv)


def halves_kernel(pos_ref, *refs):
    for index in range(4):
        keep, came, out = refs[index], refs[4 + index], refs[8 + index]
        out[...] = (keep[0].astype(F32) + came[0].astype(F32)).astype(out.dtype)


def halves(pos, keep, came):
    _, rounds, channels, width = keep.shape
    rows = channels // 2
    specs = [
        pl.BlockSpec((1, rounds, rows, width), lambda i, pos, f=f, g=g: (f, 0, pos[1] ^ g, 0))
        for f in range(2)
        for g in range(2)
    ]
    out_spec = pl.BlockSpec((rounds, rows, width), lambda i, pos: (0, 0, 0))
    return pl.pallas_call(
        halves_kernel,
        grid_spec=pltpu.PrefetchScalarGridSpec(
            num_scalar_prefetch=1, grid=(1,), in_specs=specs * 2, out_specs=[out_spec] * 4
        ),
        out_shape=[jax.ShapeDtypeStruct((rounds, rows, width), t) for t in (F32, BF16, BF16, BF16)],
        compiler_params=pltpu.CompilerParams(vmem_limit_bytes=32 << 20),
        name="halves",
    )(pos, *([keep] * 4), *([came] * 4))


def total_kernel(first, *refs):
    result = first[...]
    for ref in refs[:-1]:
        result = result + ref[...].astype(F32)
    refs[-1][...] = result.astype(refs[-1].dtype)


def total(first, *others):
    return pl.pallas_call(
        total_kernel,
        out_shape=jax.ShapeDtypeStruct(first.shape, BF16),
        name="total",
    )(first, *others)


def finish_kernel(normalizer, pos_ref, own_ref, behind_ref, *refs):
    member = pos_ref[0]
    out = refs[-1]
    for distance in range(ROUNDS):
        here = own_ref[distance].astype(F32)
        result = jnp.where(distance < member, here, behind_ref[distance].astype(F32))
        for ref in refs[:-1]:
            result = result + ref[distance].astype(F32)
        out[:, distance, :] = jnp.transpose(result * normalizer)[:LAGS]


def finish(pos, own, behind, terms, normalizer):
    width = own.shape[1]
    return pl.pallas_call(
        functools.partial(finish_kernel, normalizer),
        in_specs=[pl.BlockSpec(memory_space=pltpu.SMEM)]
        + [pl.BlockSpec(memory_space=pltpu.VMEM)] * (2 + len(terms)),
        out_shape=jax.ShapeDtypeStruct((LAGS, ROUNDS, width), F32),
        name="finish",
    )(pos, own, behind, *terms)


def make_tables(channels, freq_total, freq_local):
    half = 3 * channels // 4
    wave = 2 * np.arange(half) + 1
    period = 4 * half
    fwd_angle = 2.0 * np.pi / period * ((wave[:, None] * np.arange(channels)[None, :]) % period)
    fwd = np.concatenate([np.cos(fwd_angle), np.sin(fwd_angle)], axis=0)
    inv_angle = 2.0 * np.pi / period * ((wave[:, None] * (np.arange(channels) - channels // 2)[None, :]) % period)
    inv = np.concatenate([np.cos(inv_angle), -np.sin(inv_angle)], axis=0).T
    width = -(-LAGS // LANES) * LANES
    bins = freq_local // (GROUP * PARTS)
    tau = np.arange(LAGS) - (LAGS - 1) // 2
    lag_angle = np.pi / freq_total * ((np.arange(freq_total)[:, None] * tau[None, :]) % (2 * freq_total))
    lag_angle = lag_angle.reshape(freq_total // bins, bins, LAGS)
    lag = np.zeros((freq_total // bins, 2 * LANES, width), np.float64)
    lag[:, :bins, :LAGS] = np.cos(lag_angle)
    lag[:, LANES : LANES + bins, :LAGS] = -np.sin(lag_angle)
    return tuple(table.astype(ml_dtypes.bfloat16) for table in (fwd, lag, inv))


def on_device(n_frq, spectra, channel_valid):
    _, channels, windows, freq_local = spectra.shape
    n_blk = lax.axis_size("blk")
    freq_total = freq_local * n_frq
    fwd, lag, inv = make_tables(channels, freq_total, freq_local)
    tables = (jnp.asarray(fwd), jnp.asarray(lag), jnp.asarray(inv))
    normalizer = 1.0 / math.sqrt(windows * channels * freq_total) / (3 * channels // 2)
    member = lax.rem(lax.axis_index("blk"), GROUP)
    side = lax.axis_index("frq")
    pos = jnp.stack([member, side]).astype(jnp.int32)
    valid = channel_valid[None, :]
    bins = freq_local // (GROUP * PARTS)
    if bins != LANES:
        split = spectra.reshape(2, channels, windows, GROUP * PARTS, bins)
        split = jnp.pad(split, ((0, 0),) * 4 + ((0, LANES - bins),))
        spectra = split.reshape(2, channels, windows, GROUP * PARTS * LANES)

    def move(value, target):
        pairs = [(i, target(i)) for i in range(n_blk) if 0 <= target(i) < n_blk]
        return lax.ppermute(value, "blk", pairs)

    def swap(value, flip):
        return move(value, lambda i: i ^ flip)

    y02, y03 = whiten(spectra, valid, pos, [[(2, 0)], [(3, 0)]])
    y02_came = swap(y02, 2)
    y03_came = swap(y03, 3)
    own0, own1, core0, core1, core, y12, y13 = whiten(
        spectra,
        valid,
        after(pos, y02),
        [[(0, 0)], [(0, 1)], [(1, 0)], [(1, 1)], [(1, 0), (1, 1)], [(2, 1)], [(3, 1)]],
    )
    core_came = swap(core, 1)
    n00 = move(own0, lambda i: i - GROUP)
    n10 = move(own1, lambda i: i + GROUP)
    n01 = move(after(core0, core_came), lambda i: (i ^ 1) - GROUP)
    n11 = move(after(core1, n10), lambda i: (i ^ 1) + GROUP)
    y12_came = swap(after(y12, y02_came), 2)
    y13_came = swap(after(y13, y03_came), 3)
    far02 = move(after(y02_came, n00), lambda i: i - GROUP)
    far03 = move(after(y03_came, n01), lambda i: i - GROUP)
    far12 = move(after(y12_came, n11), lambda i: i + GROUP)
    far13 = move(y13_came, lambda i: i + GROUP)

    blocks0 = [(own0, 0), (core_came, 0), (y02_came, 0), (y03_came, 0), (n00, 0), (n01, 0), (far02, 0), (far03, 0)]
    blocks1 = [(own1, 0), (core_came, 1), (y12_came, 0), (y13_came, 0), (n10, 0), (n11, 0), (far12, 0), (far13, 0)]
    keep0, send0 = correlate(after(pos, y12_came, n11), 0, blocks0, tables)
    came0 = swap(send0, 1)

    if n_frq == 2:

        def both(value, flip, cross):
            flat = [(i, x) for i in range(n_blk) for x in range(2)]
            pairs = [(2 * i + x, 2 * (i ^ flip) + (x ^ cross)) for i, x in flat]
            return lax.ppermute(value, ("blk", "frq"), pairs)

        def spread(other, far_mine, far_other):
            return both(other, 0, 1), both(far_mine, 2, 0), both(far_other, 2, 1)

        mine0, *rest = halves(after(pos, far13), keep0, came0)
        rest = spread(*rest)
        keep1, send1 = correlate(pos, 1, blocks1, tables)
        sum0 = total(mine0, *rest)
        behind = move(sum0, lambda i: i + GROUP)
        mine1, *rest = halves(pos, keep1, swap(send1, 1))
        terms = (mine1, *spread(*rest))
    else:

        def spread(keep, came):
            both = keep.astype(F32) + came.astype(F32)
            mine = both[0] + swap(both[1].astype(BF16), 2).astype(F32)
            return lax.psum_scatter(mine, "frq", scatter_dimension=1, tiled=True)

        sum0 = spread(keep0, came0).astype(BF16)
        behind = move(sum0, lambda i: i + GROUP)
        keep1, send1 = correlate(pos, 1, blocks1, tables)
        terms = (spread(keep1, swap(send1, 1)),)
    stacked = finish(pos, sum0, behind, terms, normalizer)
    return jnp.transpose(stacked, (1, 0, 2))[None]


def solution(mesh):
    return jax.shard_map(
        functools.partial(on_device, mesh.shape["frq"]),
        mesh=mesh,
        in_specs=(P(None, "blk", None, "frq"), P("blk")),
        out_specs=P("blk", None, None, "frq"),
        check_vma=False,
    )
```

```python
import functools
import math

import jax
import jax.numpy as jnp
import ml_dtypes
import numpy as np
from jax import lax
from jax.experimental import pallas as pl
from jax.experimental.pallas import tpu as pltpu
from jax.sharding import PartitionSpec as P

LAGS = 201
ROUNDS = 4
GROUP = 4
PARTS = 2
LANES = 128
F32, BF16 = jnp.float32, jnp.bfloat16


def after(value, *others):
    return lax.optimization_barrier((value, others))[0]


def pair_list():
    pairs = []
    for own in range(GROUP):
        for distance in range(1, ROUNDS + 1):
            far = own - distance
            if far >= 0:
                pairs.append((own, far))
            elif far + GROUP >= 2:
                pairs.append((own, far + GROUP + 2))
            else:
                pairs.append((own + 6, far + GROUP))
    return pairs


def pieces_of(items):
    return sorted({piece for item in items for piece in item})


def whiten_kernel(items, pos_ref, valid_ref, spectra_ref, *refs):
    outs, held = refs[:-1], refs[-1]
    _, tile, windows, freqs = spectra_ref.shape
    parts = freqs // (GROUP * LANES)
    place = (tile, valid_ref.shape[1])
    row = lax.broadcasted_iota(jnp.int32, place, 0) + pl.program_id(0) * tile
    here = row == lax.broadcasted_iota(jnp.int32, place, 1)
    valid = jnp.sum(jnp.where(here, valid_ref[...].astype(F32), 0.0), axis=1, keepdims=True)
    for at, piece in enumerate(pieces_of(items)):
        lanes = pl.ds(pl.multiple_of(((pos_ref[0] ^ piece[0]) * parts + piece[1]) * LANES, LANES), LANES)
        for half in range(2):
            held[at, half] = spectra_ref[half, :, :, lanes].reshape(tile * windows, LANES).astype(F32)
        values = [[held[at, half, pl.ds(w, tile, stride=windows), :] for half in range(2)] for w in range(windows)]
        power = values[0][0] * values[0][0] + values[0][1] * values[0][1]
        for real, imag in values[1:]:
            power = power + (real * real + imag * imag)
        scale = valid / jnp.maximum(jnp.sqrt(power * (1.0 / windows)), 0.5)
        for w in range(windows):
            both = jnp.concatenate([values[w][half] * scale for half in range(2)], axis=1).astype(BF16)
            for item, out in zip(items, outs):
                for index, wanted in enumerate(item):
                    if wanted == piece:
                        out[index, w] = both


def whiten(spectra, valid, pos, items):
    _, channels, windows, freqs = spectra.shape
    tile = min(64, channels)
    count = len(pieces_of(items))
    in_specs = [
        pl.BlockSpec((1, channels), lambda i, pos: (0, 0)),
        pl.BlockSpec((2, tile, windows, freqs), lambda i, pos: (0, i, 0, 0)),
    ]
    out_specs = [pl.BlockSpec((len(item), windows, tile, 2 * LANES), lambda i, pos: (0, 0, i, 0)) for item in items]
    return pl.pallas_call(
        functools.partial(whiten_kernel, items),
        grid_spec=pltpu.PrefetchScalarGridSpec(
            num_scalar_prefetch=1,
            grid=(channels // tile,),
            in_specs=in_specs,
            out_specs=out_specs,
            scratch_shapes=[pltpu.VMEM((count, 2, tile * windows, LANES), F32)],
        ),
        out_shape=[jax.ShapeDtypeStruct((len(item), windows, channels, 2 * LANES), BF16) for item in items],
        compiler_params=pltpu.CompilerParams(vmem_limit_bytes=56 << 20),
        cost_estimate=pl.CostEstimate(flops=0, bytes_accessed=1000, transcendentals=0),
        name="whiten",
    )(pos, valid, spectra)


def correlate_kernel(pairs, places, part, pos_ref, *refs):
    count = 2 * GROUP
    blocks, before = refs[:count], refs[count:-16]
    fwd_in, lag_in, inv_in, keep_out, send_out = refs[-16:-11]
    held, held_before, fwd_ref, lag_ref, inv_ref, hat, plus, cross, turned, result, sem = refs[-11:]
    member = pos_ref[0]
    half = fwd_ref.shape[0] // 2
    windows = held.shape[1]

    def load(index, source, target):
        copy = pltpu.make_async_copy(source, target, sem.at[index])
        copy.start()
        return copy

    loads = [load(count, fwd_in, fwd_ref)]
    loads += [load(index, blocks[index].at[places[index]], held.at[index]) for index in range(count)]
    later = [
        load(count + 1, inv_in, inv_ref),
        load(count + 2, lag_in.at[(pos_ref[1] * GROUP + member) * PARTS + part], lag_ref),
    ]
    later += [load(count + 3 + index, source, held_before.at[index]) for index, source in enumerate(before)]
    loads[0].wait()
    for index in range(count):
        slot = member ^ (index % GROUP)
        if index >= GROUP:
            slot = jnp.where(slot < 2, slot + 6, slot + 2)
        loads[1 + index].wait()
        for w in range(windows):
            terms = jnp.dot(fwd_ref[...], held[index, w], preferred_element_type=F32)
            cos_r, cos_i = terms[:half, :LANES], terms[:half, LANES:]
            sin_r, sin_i = terms[half:, :LANES], terms[half:, LANES:]
            hat[slot, w, 0] = cos_r + sin_i
            hat[slot, w, 1] = cos_i - sin_r
            hat[slot, w, 2] = cos_r - sin_i
            hat[slot, w, 3] = cos_i + sin_r

    def products(step, carry):
        rows = pl.ds(pl.multiple_of(step * 8, 8), 8)
        odd_rows = pl.ds(pl.multiple_of(half + step * 8, 8), 8)
        for sign in range(2):
            sums = [None] * (2 * len(pairs))
            for win in range(windows):
                real = [hat[slot, win, 2 * sign, rows, :] for slot in range(count)]
                imag = [hat[slot, win, 2 * sign + 1, rows, :] for slot in range(count)]
                for n, (own, far) in enumerate(pairs):
                    part_r = real[own] * real[far] + imag[own] * imag[far]
                    part_i = imag[own] * real[far] - real[own] * imag[far]
                    sums[2 * n] = part_r if win == 0 else sums[2 * n] + part_r
                    sums[2 * n + 1] = part_i if win == 0 else sums[2 * n + 1] + part_i
            for n in range(len(pairs)):
                if sign == 0:
                    plus[2 * n], plus[2 * n + 1] = sums[2 * n], sums[2 * n + 1]
                else:
                    plus_r, plus_i = plus[2 * n], plus[2 * n + 1]
                    minus_r, minus_i = sums[2 * n], sums[2 * n + 1]
                    cross[n, rows, :LANES] = plus_r + minus_r
                    cross[n, rows, LANES:] = plus_i + minus_i
                    cross[n, odd_rows, :LANES] = plus_i - minus_i
                    cross[n, odd_rows, LANES:] = minus_r - plus_r
        return carry

    lax.fori_loop(0, half // 8, products, 0)
    for copy in later:
        copy.wait()

    def turn(n, carry):
        turned[n] = jnp.dot(inv_ref[...], cross[n].astype(BF16), preferred_element_type=F32).astype(BF16)
        return carry

    lax.fori_loop(0, len(pairs), turn, 0, unroll=8)
    stores = []
    for flip in (1, 3, 0, 2):
        for distance in range(ROUNDS):
            n = (member ^ flip) * ROUNDS + distance
            total = lax.dot_general(lag_ref[...], turned[n], (((1,), (1,)), ((), ())), preferred_element_type=F32)
            if before:
                total = total + held_before[flip % 2, flip // 2, distance].astype(F32)
            result[flip, distance] = total.astype(BF16)
        out = (keep_out, send_out)[flip % 2].at[flip // 2]
        stores.append(pltpu.make_async_copy(result.at[flip], out, sem.at[count + 5 + flip]))
        stores[-1].start()
    for copy in stores:
        copy.wait()


def correlate(pos, part, blocks, tables, before=()):
    fwd, lag, inv = tables
    _, windows, channels, lanes = blocks[0][0].shape
    rows = lag.shape[1]
    pairs = pair_list()
    half = fwd.shape[0] // 2
    places = [place for _, place in blocks]
    shape = (2, ROUNDS, rows, channels)
    anywhere = pl.BlockSpec(memory_space=pl.ANY)
    return pl.pallas_call(
        functools.partial(correlate_kernel, pairs, places, part),
        in_specs=[pl.BlockSpec(memory_space=pltpu.SMEM)] + [anywhere] * (len(blocks) + len(before) + 3),
        out_specs=[anywhere, anywhere],
        scratch_shapes=[
            pltpu.VMEM((2 * GROUP, windows, channels, lanes), BF16),
            pltpu.VMEM((2, *shape), BF16),
            pltpu.VMEM(fwd.shape, BF16),
            pltpu.VMEM(lag.shape[1:], BF16),
            pltpu.VMEM(inv.shape, BF16),
            pltpu.VMEM((2 * GROUP, windows, 4, half, LANES), F32),
            pltpu.VMEM((2 * len(pairs), 8, LANES), F32),
            pltpu.VMEM((len(pairs), 2 * half, 2 * LANES), F32),
            pltpu.VMEM((len(pairs), channels, 2 * LANES), BF16),
            pltpu.VMEM((GROUP, *shape[1:]), BF16),
            pltpu.SemaphoreType.DMA((2 * GROUP + 9,)),
        ],
        out_shape=[jax.ShapeDtypeStruct(shape, BF16)] * 2,
        compiler_params=pltpu.CompilerParams(vmem_limit_bytes=60 << 20),
        cost_estimate=pl.CostEstimate(flops=0, bytes_accessed=1000, transcendentals=0),
        name="correlate",
    )(pos, *[array for array, _ in blocks], *before, fwd, lag, inv)


def halves_kernel(pos_ref, *refs):
    for index in range(4):
        keep, came, out = refs[index], refs[4 + index], refs[8 + index]
        out[...] = (keep[0].astype(F32) + came[0].astype(F32)).astype(out.dtype)


def halves(pos, keep, came):
    _, rounds, rows, channels = keep.shape
    width = channels // 2
    specs = [
        pl.BlockSpec((1, rounds, rows, width), lambda i, pos, f=f, g=g: (f, 0, 0, pos[1] ^ g))
        for f in range(2)
        for g in range(2)
    ]
    out_spec = pl.BlockSpec((rounds, rows, width), lambda i, pos: (0, 0, 0))
    return pl.pallas_call(
        halves_kernel,
        grid_spec=pltpu.PrefetchScalarGridSpec(
            num_scalar_prefetch=1, grid=(1,), in_specs=specs * 2, out_specs=[out_spec] * 4
        ),
        out_shape=[jax.ShapeDtypeStruct((rounds, rows, width), t) for t in (F32, BF16, BF16, BF16)],
        compiler_params=pltpu.CompilerParams(vmem_limit_bytes=16 << 20),
        name="halves",
    )(pos, *([keep] * 4), *([came] * 4))


def total_kernel(*refs):
    *terms, out, back = refs
    for distance in range(ROUNDS):
        result = terms[0][distance].astype(F32)
        for term in terms[1:]:
            result = result + term[distance].astype(F32)
        out[distance] = result
        if distance >= 2:
            back[distance - 2] = result.astype(BF16)


def total(*terms):
    shape = terms[0].shape
    return pl.pallas_call(
        total_kernel,
        out_shape=[jax.ShapeDtypeStruct(shape, F32), jax.ShapeDtypeStruct((2, *shape[1:]), BF16)],
        compiler_params=pltpu.CompilerParams(vmem_limit_bytes=16 << 20),
        name="total",
    )(*terms)


def finish_kernel(normalizer, pos_ref, own_ref, behind_ref, out):
    member = pos_ref[0]
    for distance in range(ROUNDS):
        result = own_ref[distance]
        if distance >= 2:
            result = jnp.where(distance < member + 2, result, behind_ref[distance - 2].astype(F32))
        out[:, distance, :] = (result * normalizer)[:LAGS]


def finish(pos, own, behind, normalizer):
    return pl.pallas_call(
        functools.partial(finish_kernel, normalizer),
        in_specs=[pl.BlockSpec(memory_space=pltpu.SMEM)] + [pl.BlockSpec(memory_space=pltpu.VMEM)] * 2,
        out_shape=jax.ShapeDtypeStruct((LAGS, ROUNDS, own.shape[2]), F32),
        compiler_params=pltpu.CompilerParams(vmem_limit_bytes=16 << 20),
        name="finish",
    )(pos, own, behind)


def make_tables(channels, freq_total, freq_local):
    half = 3 * channels // 4
    wave = 2 * np.arange(half) + 1
    period = 4 * half
    fwd_angle = 2.0 * np.pi / period * ((wave[:, None] * np.arange(channels)[None, :]) % period)
    fwd = np.concatenate([np.cos(fwd_angle), np.sin(fwd_angle)], axis=0)
    inv_angle = 2.0 * np.pi / period * ((wave[:, None] * (np.arange(channels) - channels // 2)[None, :]) % period)
    inv = np.concatenate([np.cos(inv_angle), -np.sin(inv_angle)], axis=0).T
    rows = -(-LAGS // 16) * 16
    bins = freq_local // (GROUP * PARTS)
    tau = np.arange(LAGS) - (LAGS - 1) // 2
    lag_angle = np.pi / freq_total * ((tau[:, None] * np.arange(freq_total)[None, :]) % (2 * freq_total))
    lag_angle = lag_angle.reshape(LAGS, freq_total // bins, bins).transpose(1, 0, 2)
    lag = np.zeros((freq_total // bins, rows, 2 * LANES), np.float64)
    lag[:, :LAGS, :bins] = np.cos(lag_angle)
    lag[:, :LAGS, LANES : LANES + bins] = -np.sin(lag_angle)
    return tuple(table.astype(ml_dtypes.bfloat16) for table in (fwd, lag, inv))


def on_device(n_frq, spectra, channel_valid):
    _, channels, windows, freq_local = spectra.shape
    n_blk = lax.axis_size("blk")
    freq_total = freq_local * n_frq
    fwd, lag, inv = make_tables(channels, freq_total, freq_local)
    tables = (jnp.asarray(fwd), jnp.asarray(lag), jnp.asarray(inv))
    normalizer = 1.0 / math.sqrt(windows * channels * freq_total) / (3 * channels // 2)
    member = lax.rem(lax.axis_index("blk"), GROUP)
    side = lax.axis_index("frq")
    pos = jnp.stack([member, side]).astype(jnp.int32)
    valid = channel_valid[None, :]
    bins = freq_local // (GROUP * PARTS)
    if bins != LANES:
        split = spectra.reshape(2, channels, windows, GROUP * PARTS, bins)
        split = jnp.pad(split, ((0, 0),) * 4 + ((0, LANES - bins),))
        spectra = split.reshape(2, channels, windows, GROUP * PARTS * LANES)

    def move(value, target):
        pairs = [(i, target(i)) for i in range(n_blk) if 0 <= target(i) < n_blk]
        return lax.ppermute(value, "blk", pairs)

    def swap(value, flip):
        return move(value, lambda i: i ^ flip)

    def up(i):
        return i % GROUP >= 2

    def forward(value):
        return move(value, lambda i: i - GROUP if up(i) else i + GROUP)

    def near(value, flip):
        return move(value, lambda i: (i ^ flip) + (GROUP if up(i) else -GROUP))

    y02, y03, y12, y13, core, core0, core1, own0, own1 = whiten(
        spectra,
        valid,
        pos,
        [[(2, 0)], [(3, 0)], [(2, 1)], [(3, 1)], [(1, 0), (1, 1)], [(1, 0)], [(1, 1)], [(0, 0)], [(0, 1)]],
    )
    y02_came = swap(y02, 2)
    y03_came = swap(y03, 3)
    core_came = swap(core, 1)
    near00 = near(own0, 0)
    near01 = near(core0, 1)
    y12_came = swap(after(y12, y02_came, core_came), 2)
    far02 = forward(after(y02_came, core_came))
    near10 = near(after(own1, near00), 0)
    y13_came = swap(after(y13, y03_came, near00), 3)
    far03 = forward(after(y03_came, near00, far02))
    near11 = near(after(core1, near01), 1)
    far12 = forward(after(y12_came, far02))
    far13 = forward(after(y13_came, far03))

    blocks0 = [(own0, 0), (core_came, 0), (y02_came, 0), (y03_came, 0), (near00, 0), (near01, 0), (far02, 0), (far03, 0)]
    blocks1 = [(own1, 0), (core_came, 1), (y12_came, 0), (y13_came, 0), (near10, 0), (near11, 0), (far12, 0), (far13, 0)]
    partial = correlate(after(pos, y13_came), 0, blocks0, tables)
    keep, send = correlate(pos, 1, blocks1, tables, partial)
    came = swap(send, 1)

    if n_frq == 2:

        def both(value, flip, cross):
            flat = [(i, x) for i in range(n_blk) for x in range(2)]
            pairs = [(2 * i + x, 2 * (i ^ flip) + (x ^ cross)) for i, x in flat]
            return lax.ppermute(value, ("blk", "frq"), pairs)

        mine, other, far_mine, far_other = halves(pos, keep, came)
        terms = [mine, both(other, 0, 1), both(far_mine, 2, 0), both(far_other, 2, 1)]
    else:
        both = keep.astype(F32) + came.astype(F32)
        both = both[0] + swap(both[1].astype(BF16), 2).astype(F32)
        terms = [lax.psum_scatter(both, "frq", scatter_dimension=2, tiled=True)]
    result, back = total(*terms)
    behind = move(back, lambda i: n_blk if up(i) else i + GROUP)
    stacked = finish(pos, result, behind, normalizer)
    return jnp.transpose(stacked, (1, 0, 2))[None]


def solution(mesh):
    return jax.shard_map(
        functools.partial(on_device, mesh.shape["frq"]),
        mesh=mesh,
        in_specs=(P(None, "blk", None, "frq"), P("blk")),
        out_specs=P("blk", None, None, "frq"),
        check_vma=False,
    )
```

```python
import functools
import math

import jax
import jax.numpy as jnp
import ml_dtypes
import numpy as np
from jax import lax
from jax.experimental import pallas as pl
from jax.experimental.pallas import tpu as pltpu
from jax.sharding import PartitionSpec as P

LAGS = 201
ROUNDS = 4
GROUP = 4
PARTS = 2
LANES = 128
F32, BF16 = jnp.float32, jnp.bfloat16


def after(value, *others):
    return lax.optimization_barrier((value, others))[0]


def pair_list():
    pairs = []
    for own in range(GROUP):
        for distance in range(1, ROUNDS + 1):
            far = own - distance
            if far >= 0:
                pairs.append((own, far))
            elif far + GROUP >= 2:
                pairs.append((own, far + GROUP + 2))
            else:
                pairs.append((own + 6, far + GROUP))
    return pairs


def pieces_of(items):
    return sorted({piece for item in items for piece in item})


def whiten_kernel(items, tile, valid_ref, spectra_ref, *refs):
    outs, (raw, held, ready, load_sem, store_sem) = refs[: len(items)], refs[len(items) :]
    member = lax.rem(lax.axis_index("blk"), GROUP)
    _, channels, windows, freqs = spectra_ref.shape
    parts = freqs // (GROUP * LANES)
    pieces = pieces_of(items)
    steps = channels // tile

    def load(step):
        rows = pl.ds(pl.multiple_of(step * tile, tile), tile)
        return pltpu.make_async_copy(spectra_ref.at[:, rows], raw.at[:, rows], load_sem.at[step])

    def stores(step):
        rows = pl.ds(pl.multiple_of(step * tile, tile), tile)
        copies = []
        for out, item in zip(outs, items):
            for index, piece in enumerate(item):
                source = ready.at[pieces.index(piece), :, rows]
                copies.append(pltpu.make_async_copy(source, out.at[index, :, rows], store_sem.at[step, len(copies)]))
        return copies

    for step in range(steps):
        load(step).start()

    def work(step, carry):
        load(step).wait()
        rows = pl.ds(pl.multiple_of(step * tile, tile), tile)
        place = (tile, channels)
        row = lax.broadcasted_iota(jnp.int32, place, 0) + step * tile
        here = row == lax.broadcasted_iota(jnp.int32, place, 1)
        valid = jnp.sum(jnp.where(here, valid_ref[...].astype(F32), 0.0), axis=1, keepdims=True)
        for at, (flip, part) in enumerate(pieces):
            lanes = pl.ds(pl.multiple_of(((member ^ flip) * parts + part) * LANES, LANES), LANES)
            for half in range(2):
                held[at, half] = raw[half, rows, :, lanes].reshape(tile * windows, LANES).astype(F32)
            values = [
                [held[at, half, pl.ds(w, tile, stride=windows), :] for half in range(2)] for w in range(windows)
            ]
            power = values[0][0] * values[0][0] + values[0][1] * values[0][1]
            for real, imag in values[1:]:
                power = power + (real * real + imag * imag)
            scale = valid / jnp.maximum(jnp.sqrt(power * (1.0 / windows)), 0.5)
            for w in range(windows):
                both = jnp.concatenate([values[w][half] * scale for half in range(2)], axis=1)
                ready[at, w, rows, :] = both.astype(BF16)
        for copy in stores(step):
            copy.start()
        return carry

    lax.fori_loop(0, steps, work, 0)

    def drain(step, carry):
        for copy in stores(step):
            copy.wait()
        return carry

    lax.fori_loop(0, steps, drain, 0)


def whiten(spectra, valid, items):
    _, channels, windows, _ = spectra.shape
    tile = min(32, channels)
    count = len(pieces_of(items))
    anywhere = pl.BlockSpec(memory_space=pl.ANY)
    return pl.pallas_call(
        functools.partial(whiten_kernel, items, tile),
        in_specs=[pl.BlockSpec(memory_space=pltpu.VMEM), anywhere],
        out_specs=[anywhere] * len(items),
        scratch_shapes=[
            pltpu.VMEM(spectra.shape, BF16),
            pltpu.VMEM((count, 2, tile * windows, LANES), F32),
            pltpu.VMEM((count, windows, channels, 2 * LANES), BF16),
            pltpu.SemaphoreType.DMA((channels // tile,)),
            pltpu.SemaphoreType.DMA((channels // tile, sum(len(item) for item in items))),
        ],
        out_shape=[jax.ShapeDtypeStruct((len(item), windows, channels, 2 * LANES), BF16) for item in items],
        compiler_params=pltpu.CompilerParams(vmem_limit_bytes=56 << 20),
        cost_estimate=pl.CostEstimate(flops=0, bytes_accessed=1000, transcendentals=0),
        name="whiten",
    )(valid, spectra)


def correlate_kernel(pairs, places, part, pos_ref, *refs):
    count, pieces = 2 * GROUP, sum(len(block) for block in places)
    blocks, before = iter(refs[:pieces]), refs[pieces:-16]
    fwd_in, lag_in, inv_in, keep_out, send_out = refs[-16:-11]
    held, held_before, fwd_ref, lag_ref, inv_ref, hat, plus, cross, turned, result, sem = refs[-11:]
    member = pos_ref[0]
    half = fwd_ref.shape[0] // 2
    windows = held.shape[1]

    def load(index, source, target):
        copy = pltpu.make_async_copy(source, target, sem.at[index])
        copy.start()
        return copy

    fwd_load = load(pieces, fwd_in, fwd_ref)
    loads = []
    for index, block in enumerate(places):
        first = 0
        for place in block:
            source = next(blocks).at[place]
            target = held.at[index, pl.ds(first, source.shape[0])]
            loads.append((index, load(len(loads), source, target)))
            first += source.shape[0]
    later = [
        load(pieces + 1, inv_in, inv_ref),
        load(pieces + 2, lag_in.at[(pos_ref[1] * GROUP + member) * PARTS + part], lag_ref),
    ]
    later += [load(pieces + 3 + index, source, held_before.at[index]) for index, source in enumerate(before)]
    fwd_load.wait()
    for index in range(count):
        slot = member ^ (index % GROUP)
        if index >= GROUP:
            slot = jnp.where(slot < 2, slot + 6, slot + 2)
        for target, copy in loads:
            if target == index:
                copy.wait()
        for w in range(windows):
            terms = jnp.dot(fwd_ref[...], held[index, w], preferred_element_type=F32)
            cos_r, cos_i = terms[:half, :LANES], terms[:half, LANES:]
            sin_r, sin_i = terms[half:, :LANES], terms[half:, LANES:]
            hat[slot, w, 0] = cos_r + sin_i
            hat[slot, w, 1] = cos_i - sin_r
            hat[slot, w, 2] = cos_r - sin_i
            hat[slot, w, 3] = cos_i + sin_r

    def products(step, carry):
        rows = pl.ds(pl.multiple_of(step * 8, 8), 8)
        odd_rows = pl.ds(pl.multiple_of(half + step * 8, 8), 8)
        for sign in range(2):
            sums = [None] * (2 * len(pairs))
            for win in range(windows):
                real = [hat[slot, win, 2 * sign, rows, :] for slot in range(count)]
                imag = [hat[slot, win, 2 * sign + 1, rows, :] for slot in range(count)]
                for n, (own, far) in enumerate(pairs):
                    part_r = real[own] * real[far] + imag[own] * imag[far]
                    part_i = imag[own] * real[far] - real[own] * imag[far]
                    sums[2 * n] = part_r if win == 0 else sums[2 * n] + part_r
                    sums[2 * n + 1] = part_i if win == 0 else sums[2 * n + 1] + part_i
            for n in range(len(pairs)):
                if sign == 0:
                    plus[2 * n], plus[2 * n + 1] = sums[2 * n], sums[2 * n + 1]
                else:
                    plus_r, plus_i = plus[2 * n], plus[2 * n + 1]
                    minus_r, minus_i = sums[2 * n], sums[2 * n + 1]
                    cross[n, rows, :LANES] = plus_r + minus_r
                    cross[n, rows, LANES:] = plus_i + minus_i
                    cross[n, odd_rows, :LANES] = plus_i - minus_i
                    cross[n, odd_rows, LANES:] = minus_r - plus_r
        return carry

    lax.fori_loop(0, half // 8, products, 0)
    for copy in later:
        copy.wait()

    def turn(n, carry):
        turned[n] = jnp.dot(inv_ref[...], cross[n].astype(BF16), preferred_element_type=F32).astype(BF16)
        return carry

    lax.fori_loop(0, len(pairs), turn, 0, unroll=8)
    stores = []
    for flip in (1, 3, 0, 2):
        for distance in range(ROUNDS):
            n = (member ^ flip) * ROUNDS + distance
            total = lax.dot_general(lag_ref[...], turned[n], (((1,), (1,)), ((), ())), preferred_element_type=F32)
            if before:
                total = total + held_before[flip % 2, flip // 2, distance].astype(F32)
            result[flip, distance] = total.astype(BF16)
        out = (keep_out, send_out)[flip % 2].at[flip // 2]
        stores.append(pltpu.make_async_copy(result.at[flip], out, sem.at[pieces + 5 + flip]))
        stores[-1].start()
    for copy in stores:
        copy.wait()


def correlate(pos, part, blocks, tables, before=()):
    fwd, lag, inv = tables
    windows = sum(array.shape[1] for array, _ in blocks[0])
    channels, lanes = blocks[0][0][0].shape[2:]
    rows = lag.shape[1]
    pairs = pair_list()
    half = fwd.shape[0] // 2
    places = [[place for _, place in block] for block in blocks]
    arrays = [array for block in blocks for array, _ in block]
    shape = (2, ROUNDS, rows, channels)
    anywhere = pl.BlockSpec(memory_space=pl.ANY)
    return pl.pallas_call(
        functools.partial(correlate_kernel, pairs, places, part),
        in_specs=[pl.BlockSpec(memory_space=pltpu.SMEM)] + [anywhere] * (len(arrays) + len(before) + 3),
        out_specs=[anywhere, anywhere],
        scratch_shapes=[
            pltpu.VMEM((2 * GROUP, windows, channels, lanes), BF16),
            pltpu.VMEM((2, *shape), BF16),
            pltpu.VMEM(fwd.shape, BF16),
            pltpu.VMEM(lag.shape[1:], BF16),
            pltpu.VMEM(inv.shape, BF16),
            pltpu.VMEM((2 * GROUP, windows, 4, half, LANES), F32),
            pltpu.VMEM((2 * len(pairs), 8, LANES), F32),
            pltpu.VMEM((len(pairs), 2 * half, 2 * LANES), F32),
            pltpu.VMEM((len(pairs), channels, 2 * LANES), BF16),
            pltpu.VMEM((GROUP, *shape[1:]), BF16),
            pltpu.SemaphoreType.DMA((len(arrays) + 9,)),
        ],
        out_shape=[jax.ShapeDtypeStruct(shape, BF16)] * 2,
        compiler_params=pltpu.CompilerParams(vmem_limit_bytes=62 << 20),
        cost_estimate=pl.CostEstimate(flops=0, bytes_accessed=1000, transcendentals=0),
        name="correlate",
    )(pos, *arrays, *before, fwd, lag, inv)


def halves_kernel(pos_ref, *refs):
    for index in range(4):
        keep, came, out = refs[index], refs[4 + index], refs[8 + index]
        out[...] = (keep[0].astype(F32) + came[0].astype(F32)).astype(out.dtype)


def halves(pos, keep, came):
    _, rounds, rows, channels = keep.shape
    width = channels // 2
    specs = [
        pl.BlockSpec((1, rounds, rows, width), lambda i, pos, f=f, g=g: (f, 0, 0, pos[1] ^ g))
        for f in range(2)
        for g in range(2)
    ]
    out_spec = pl.BlockSpec((rounds, rows, width), lambda i, pos: (0, 0, 0))
    return pl.pallas_call(
        halves_kernel,
        grid_spec=pltpu.PrefetchScalarGridSpec(
            num_scalar_prefetch=1, grid=(1,), in_specs=specs * 2, out_specs=[out_spec] * 4
        ),
        out_shape=[jax.ShapeDtypeStruct((rounds, rows, width), t) for t in (F32, BF16, BF16, BF16)],
        compiler_params=pltpu.CompilerParams(vmem_limit_bytes=16 << 20),
        name="halves",
    )(pos, *([keep] * 4), *([came] * 4))


def total_kernel(*refs):
    *terms, out, back = refs
    for distance in range(ROUNDS):
        result = terms[0][distance].astype(F32)
        for term in terms[1:]:
            result = result + term[distance].astype(F32)
        out[distance] = result
        if distance >= 2:
            back[distance - 2] = result.astype(BF16)


def total(*terms):
    shape = terms[0].shape
    return pl.pallas_call(
        total_kernel,
        out_shape=[jax.ShapeDtypeStruct(shape, F32), jax.ShapeDtypeStruct((2, *shape[1:]), BF16)],
        compiler_params=pltpu.CompilerParams(vmem_limit_bytes=16 << 20),
        name="total",
    )(*terms)


def finish_kernel(normalizer, pos_ref, own_ref, behind_ref, out):
    member = pos_ref[0]
    for distance in range(ROUNDS):
        result = own_ref[distance]
        if distance >= 2:
            result = jnp.where(distance < member + 2, result, behind_ref[distance - 2].astype(F32))
        out[:, distance, :] = (result * normalizer)[:LAGS]


def finish(pos, own, behind, normalizer):
    return pl.pallas_call(
        functools.partial(finish_kernel, normalizer),
        in_specs=[pl.BlockSpec(memory_space=pltpu.SMEM)] + [pl.BlockSpec(memory_space=pltpu.VMEM)] * 2,
        out_shape=jax.ShapeDtypeStruct((LAGS, ROUNDS, own.shape[2]), F32),
        compiler_params=pltpu.CompilerParams(vmem_limit_bytes=16 << 20),
        name="finish",
    )(pos, own, behind)


def make_tables(channels, freq_total, freq_local):
    half = 3 * channels // 4
    wave = 2 * np.arange(half) + 1
    period = 4 * half
    fwd_angle = 2.0 * np.pi / period * ((wave[:, None] * np.arange(channels)[None, :]) % period)
    fwd = np.concatenate([np.cos(fwd_angle), np.sin(fwd_angle)], axis=0)
    inv_angle = 2.0 * np.pi / period * ((wave[:, None] * (np.arange(channels) - channels // 2)[None, :]) % period)
    inv = np.concatenate([np.cos(inv_angle), -np.sin(inv_angle)], axis=0).T
    rows = -(-LAGS // 16) * 16
    bins = freq_local // (GROUP * PARTS)
    tau = np.arange(LAGS) - (LAGS - 1) // 2
    lag_angle = np.pi / freq_total * ((tau[:, None] * np.arange(freq_total)[None, :]) % (2 * freq_total))
    lag_angle = lag_angle.reshape(LAGS, freq_total // bins, bins).transpose(1, 0, 2)
    lag = np.zeros((freq_total // bins, rows, 2 * LANES), np.float64)
    lag[:, :LAGS, :bins] = np.cos(lag_angle)
    lag[:, :LAGS, LANES : LANES + bins] = -np.sin(lag_angle)
    return tuple(table.astype(ml_dtypes.bfloat16) for table in (fwd, lag, inv))


def on_device(n_frq, spectra, channel_valid):
    _, channels, windows, freq_local = spectra.shape
    n_blk = lax.axis_size("blk")
    freq_total = freq_local * n_frq
    fwd, lag, inv = make_tables(channels, freq_total, freq_local)
    tables = (jnp.asarray(fwd), jnp.asarray(lag), jnp.asarray(inv))
    normalizer = 1.0 / math.sqrt(windows * channels * freq_total) / (3 * channels // 2)
    member = lax.rem(lax.axis_index("blk"), GROUP)
    side = lax.axis_index("frq")
    pos = jnp.stack([member, side]).astype(jnp.int32)
    valid = channel_valid[None, :]
    bins = freq_local // (GROUP * PARTS)
    if bins != LANES:
        split = spectra.reshape(2, channels, windows, GROUP * PARTS, bins)
        split = jnp.pad(split, ((0, 0),) * 4 + ((0, LANES - bins),))
        spectra = split.reshape(2, channels, windows, GROUP * PARTS * LANES)

    def move(value, target):
        pairs = [(i, target(i)) for i in range(n_blk) if 0 <= target(i) < n_blk]
        return lax.ppermute(value, "blk", pairs)

    def swap(value, flip):
        return move(value, lambda i: i ^ flip)

    def up(i):
        return i % GROUP >= 2

    def forward(value):
        return move(value, lambda i: i - GROUP if up(i) else i + GROUP)

    def near(value, flip):
        return move(value, lambda i: (i ^ flip) + (GROUP if up(i) else -GROUP))

    y02, y03, y12, y13, core, core0, core1, own0, own1 = whiten(
        spectra,
        valid,
        [[(2, 0)], [(3, 0)], [(2, 1)], [(3, 1)], [(1, 0), (1, 1)], [(1, 0)], [(1, 1)], [(0, 0)], [(0, 1)]],
    )
    y02_came = swap(y02, 2)
    y03_came = swap(y03, 3)
    core_came = swap(core, 1)
    near00 = near(own0, 0)
    near01 = near(core0, 1)
    y12_came = swap(after(y12, y02_came, core_came), 2)
    far02 = forward(after(y02_came, core_came))
    near10 = near(after(own1, near00), 0)
    y13_came = swap(after(y13, y03_came, near00), 3)
    far03 = forward(after(y03_came, near00, far02))
    near11 = near(after(core1, near01), 1)
    far12 = forward(after(y12_came, far02))
    far13 = forward(after(y13_came, far03))

    blocks0 = [[(own0, 0)], [(core_came, 0)], [(y02_came, 0)], [(y03_came, 0)], [(near00, 0)], [(near01, 0)], [(far02, 0)], [(far03, 0)]]
    blocks1 = [[(own1, 0)], [(core_came, 1)], [(y12_came, 0)], [(y13_came, 0)], [(near10, 0)], [(near11, 0)], [(far12, 0)], [(far13, 0)]]
    partial = correlate(after(pos, y13_came), 0, blocks0, tables)
    keep, send = correlate(pos, 1, blocks1, tables, partial)
    came = swap(send, 1)

    if n_frq == 2:

        def both(value, flip, cross):
            flat = [(i, x) for i in range(n_blk) for x in range(2)]
            pairs = [(2 * i + x, 2 * (i ^ flip) + (x ^ cross)) for i, x in flat]
            return lax.ppermute(value, ("blk", "frq"), pairs)

        mine, other, far_mine, far_other = halves(pos, keep, came)
        terms = [mine, both(other, 0, 1), both(far_mine, 2, 0), both(far_other, 2, 1)]
    else:
        both = keep.astype(F32) + came.astype(F32)
        both = both[0] + swap(both[1].astype(BF16), 2).astype(F32)
        terms = [lax.psum_scatter(both, "frq", scatter_dimension=2, tiled=True)]
    result, back = total(*terms)
    behind = move(back, lambda i: n_blk if up(i) else i + GROUP)
    stacked = finish(pos, result, behind, normalizer)
    return jnp.transpose(stacked, (1, 0, 2))[None]


def solution(mesh):
    return jax.shard_map(
        functools.partial(on_device, mesh.shape["frq"]),
        mesh=mesh,
        in_specs=(P(None, "blk", None, "frq"), P("blk")),
        out_specs=P("blk", None, None, "frq"),
        check_vma=False,
    )
```

```python
import functools
import math

import jax
import jax.numpy as jnp
import ml_dtypes
import numpy as np
from jax import lax
from jax.experimental import pallas as pl
from jax.experimental.pallas import tpu as pltpu
from jax.sharding import PartitionSpec as P

LAGS = 201
ROUNDS = 4
GROUP = 4
PARTS = 2
LANES = 128
F32, BF16 = jnp.float32, jnp.bfloat16


def after(value, *others):
    return lax.optimization_barrier((value, others))[0]


def pair_list():
    pairs = []
    for own in range(GROUP):
        for distance in range(1, ROUNDS + 1):
            far = own - distance
            if far >= 0:
                pairs.append((own, far))
            elif far + GROUP >= 2:
                pairs.append((own, far + GROUP + 2))
            else:
                pairs.append((own + 6, far + GROUP))
    return pairs


def pieces_of(items):
    return sorted({piece for item in items for piece in item})


def whiten_kernel(items, tile, valid_ref, spectra_ref, *refs):
    outs, (raw, held, ready, load_sem, store_sem) = refs[: len(items)], refs[len(items) :]
    member = lax.rem(lax.axis_index("blk"), GROUP)
    _, channels, windows, freqs = spectra_ref.shape
    parts = freqs // (GROUP * LANES)
    pieces = pieces_of(items)
    steps = channels // tile

    def load(step):
        rows = pl.ds(pl.multiple_of(step * tile, tile), tile)
        return pltpu.make_async_copy(spectra_ref.at[:, rows], raw.at[:, rows], load_sem.at[step])

    def stores(step):
        rows = pl.ds(pl.multiple_of(step * tile, tile), tile)
        copies = []
        for out, item in zip(outs, items):
            for index, piece in enumerate(item):
                source = ready.at[pieces.index(piece), :, rows]
                copies.append(pltpu.make_async_copy(source, out.at[index, :, rows], store_sem.at[step, len(copies)]))
        return copies

    for step in range(steps):
        load(step).start()

    def work(step, carry):
        load(step).wait()
        rows = pl.ds(pl.multiple_of(step * tile, tile), tile)
        place = (tile, channels)
        row = lax.broadcasted_iota(jnp.int32, place, 0) + step * tile
        here = row == lax.broadcasted_iota(jnp.int32, place, 1)
        valid = jnp.sum(jnp.where(here, valid_ref[...].astype(F32), 0.0), axis=1, keepdims=True)
        for at, (flip, part) in enumerate(pieces):
            lanes = pl.ds(pl.multiple_of(((member ^ flip) * parts + part) * LANES, LANES), LANES)
            for half in range(2):
                held[at, half] = raw[half, rows, :, lanes].reshape(tile * windows, LANES).astype(F32)
            values = [
                [held[at, half, pl.ds(w, tile, stride=windows), :] for half in range(2)] for w in range(windows)
            ]
            power = values[0][0] * values[0][0] + values[0][1] * values[0][1]
            for real, imag in values[1:]:
                power = power + (real * real + imag * imag)
            scale = valid / jnp.maximum(jnp.sqrt(power * (1.0 / windows)), 0.5)
            for w in range(windows):
                both = jnp.concatenate([values[w][half] * scale for half in range(2)], axis=1)
                ready[at, w, rows, :] = both.astype(BF16)
        for copy in stores(step):
            copy.start()
        return carry

    lax.fori_loop(0, steps, work, 0)

    def drain(step, carry):
        for copy in stores(step):
            copy.wait()
        return carry

    lax.fori_loop(0, steps, drain, 0)


def whiten(spectra, valid, items):
    _, channels, windows, _ = spectra.shape
    tile = min(32, channels)
    count = len(pieces_of(items))
    anywhere = pl.BlockSpec(memory_space=pl.ANY)
    return pl.pallas_call(
        functools.partial(whiten_kernel, items, tile),
        in_specs=[pl.BlockSpec(memory_space=pltpu.VMEM), anywhere],
        out_specs=[anywhere] * len(items),
        scratch_shapes=[
            pltpu.VMEM(spectra.shape, BF16),
            pltpu.VMEM((count, 2, tile * windows, LANES), F32),
            pltpu.VMEM((count, windows, channels, 2 * LANES), BF16),
            pltpu.SemaphoreType.DMA((channels // tile,)),
            pltpu.SemaphoreType.DMA((channels // tile, sum(len(item) for item in items))),
        ],
        out_shape=[jax.ShapeDtypeStruct((len(item), windows, channels, 2 * LANES), BF16) for item in items],
        compiler_params=pltpu.CompilerParams(vmem_limit_bytes=56 << 20),
        cost_estimate=pl.CostEstimate(flops=0, bytes_accessed=1000, transcendentals=0),
        name="whiten",
    )(valid, spectra)


def correlate_kernel(pairs, places, part, pos_ref, *refs):
    count, pieces = 2 * GROUP, sum(len(block) for block in places)
    blocks, before = iter(refs[:pieces]), refs[pieces:-16]
    fwd_in, lag_in, inv_in, keep_out, send_out = refs[-16:-11]
    held, held_before, fwd_ref, lag_ref, inv_ref, hat, plus, cross, turned, result, sem = refs[-11:]
    member = pos_ref[0]
    half = fwd_ref.shape[0] // 2
    windows = held.shape[1]

    def load(index, source, target):
        copy = pltpu.make_async_copy(source, target, sem.at[index])
        copy.start()
        return copy

    fwd_load = load(pieces, fwd_in, fwd_ref)
    loads = []
    for index, block in enumerate(places):
        first = 0
        for place in block:
            source = next(blocks).at[place]
            target = held.at[index, pl.ds(first, source.shape[0])]
            loads.append((index, load(len(loads), source, target)))
            first += source.shape[0]
    later = [
        load(pieces + 1, inv_in, inv_ref),
        load(pieces + 2, lag_in.at[(pos_ref[1] * GROUP + member) * PARTS + part], lag_ref),
    ]
    later += [load(pieces + 3 + index, source, held_before.at[index]) for index, source in enumerate(before)]
    fwd_load.wait()
    for index in range(count):
        slot = member ^ (index % GROUP)
        if index >= GROUP:
            slot = jnp.where(slot < 2, slot + 6, slot + 2)
        for target, copy in loads:
            if target == index:
                copy.wait()
        for w in range(windows):
            terms = jnp.dot(fwd_ref[...], held[index, w], preferred_element_type=F32)
            cos_r, cos_i = terms[:half, :LANES], terms[:half, LANES:]
            sin_r, sin_i = terms[half:, :LANES], terms[half:, LANES:]
            hat[slot, w, 0] = cos_r + sin_i
            hat[slot, w, 1] = cos_i - sin_r
            hat[slot, w, 2] = cos_r - sin_i
            hat[slot, w, 3] = cos_i + sin_r

    def products(step, carry):
        rows = pl.ds(pl.multiple_of(step * 8, 8), 8)
        odd_rows = pl.ds(pl.multiple_of(half + step * 8, 8), 8)
        for sign in range(2):
            sums = [None] * (2 * len(pairs))
            for win in range(windows):
                real = [hat[slot, win, 2 * sign, rows, :] for slot in range(count)]
                imag = [hat[slot, win, 2 * sign + 1, rows, :] for slot in range(count)]
                for n, (own, far) in enumerate(pairs):
                    part_r = real[own] * real[far] + imag[own] * imag[far]
                    part_i = imag[own] * real[far] - real[own] * imag[far]
                    sums[2 * n] = part_r if win == 0 else sums[2 * n] + part_r
                    sums[2 * n + 1] = part_i if win == 0 else sums[2 * n + 1] + part_i
            for n in range(len(pairs)):
                if sign == 0:
                    plus[2 * n], plus[2 * n + 1] = sums[2 * n], sums[2 * n + 1]
                else:
                    plus_r, plus_i = plus[2 * n], plus[2 * n + 1]
                    minus_r, minus_i = sums[2 * n], sums[2 * n + 1]
                    cross[n, rows, :LANES] = plus_r + minus_r
                    cross[n, rows, LANES:] = plus_i + minus_i
                    cross[n, odd_rows, :LANES] = plus_i - minus_i
                    cross[n, odd_rows, LANES:] = minus_r - plus_r
        return carry

    lax.fori_loop(0, half // 8, products, 0)
    for copy in later:
        copy.wait()

    def turn(n, carry):
        turned[n] = jnp.dot(inv_ref[...], cross[n].astype(BF16), preferred_element_type=F32).astype(BF16)
        return carry

    lax.fori_loop(0, len(pairs), turn, 0, unroll=8)
    stores = []
    for flip in (1, 3, 0, 2):
        for distance in range(ROUNDS):
            n = (member ^ flip) * ROUNDS + distance
            total = lax.dot_general(lag_ref[...], turned[n], (((1,), (1,)), ((), ())), preferred_element_type=F32)
            if before:
                total = total + held_before[flip % 2, flip // 2, distance].astype(F32)
            result[flip, distance] = total.astype(BF16)
        out = (keep_out, send_out)[flip % 2].at[flip // 2]
        stores.append(pltpu.make_async_copy(result.at[flip], out, sem.at[pieces + 5 + flip]))
        stores[-1].start()
    for copy in stores:
        copy.wait()


def correlate(pos, part, blocks, tables, before=()):
    fwd, lag, inv = tables
    windows = sum(array.shape[1] for array, _ in blocks[0])
    channels, lanes = blocks[0][0][0].shape[2:]
    rows = lag.shape[1]
    pairs = pair_list()
    half = fwd.shape[0] // 2
    places = [[place for _, place in block] for block in blocks]
    arrays = [array for block in blocks for array, _ in block]
    shape = (2, ROUNDS, rows, channels)
    anywhere = pl.BlockSpec(memory_space=pl.ANY)
    return pl.pallas_call(
        functools.partial(correlate_kernel, pairs, places, part),
        in_specs=[pl.BlockSpec(memory_space=pltpu.SMEM)] + [anywhere] * (len(arrays) + len(before) + 3),
        out_specs=[anywhere, anywhere],
        scratch_shapes=[
            pltpu.VMEM((2 * GROUP, windows, channels, lanes), BF16),
            pltpu.VMEM((2, *shape), BF16),
            pltpu.VMEM(fwd.shape, BF16),
            pltpu.VMEM(lag.shape[1:], BF16),
            pltpu.VMEM(inv.shape, BF16),
            pltpu.VMEM((2 * GROUP, windows, 4, half, LANES), F32),
            pltpu.VMEM((2 * len(pairs), 8, LANES), F32),
            pltpu.VMEM((len(pairs), 2 * half, 2 * LANES), F32),
            pltpu.VMEM((len(pairs), channels, 2 * LANES), BF16),
            pltpu.VMEM((GROUP, *shape[1:]), BF16),
            pltpu.SemaphoreType.DMA((len(arrays) + 9,)),
        ],
        out_shape=[jax.ShapeDtypeStruct(shape, BF16)] * 2,
        compiler_params=pltpu.CompilerParams(vmem_limit_bytes=62 << 20),
        cost_estimate=pl.CostEstimate(flops=0, bytes_accessed=1000, transcendentals=0),
        name="correlate",
    )(pos, *arrays, *before, fwd, lag, inv)


def halves_kernel(pos_ref, *refs):
    for index in range(4):
        keep, came, out = refs[index], refs[4 + index], refs[8 + index]
        out[...] = (keep[0].astype(F32) + came[0].astype(F32)).astype(out.dtype)


def halves(pos, keep, came):
    _, rounds, rows, channels = keep.shape
    width = channels // 2
    specs = [
        pl.BlockSpec((1, rounds, rows, width), lambda i, pos, f=f, g=g: (f, 0, 0, pos[1] ^ g))
        for f in range(2)
        for g in range(2)
    ]
    out_spec = pl.BlockSpec((rounds, rows, width), lambda i, pos: (0, 0, 0))
    return pl.pallas_call(
        halves_kernel,
        grid_spec=pltpu.PrefetchScalarGridSpec(
            num_scalar_prefetch=1, grid=(1,), in_specs=specs * 2, out_specs=[out_spec] * 4
        ),
        out_shape=[jax.ShapeDtypeStruct((rounds, rows, width), t) for t in (F32, BF16, BF16, BF16)],
        compiler_params=pltpu.CompilerParams(vmem_limit_bytes=16 << 20),
        name="halves",
    )(pos, *([keep] * 4), *([came] * 4))


def total_kernel(*refs):
    *terms, out, back = refs
    for distance in range(ROUNDS):
        result = terms[0][distance].astype(F32)
        for term in terms[1:]:
            result = result + term[distance].astype(F32)
        out[distance] = result
        if distance >= 2:
            back[distance - 2] = result.astype(BF16)


def total(*terms):
    shape = terms[0].shape
    return pl.pallas_call(
        total_kernel,
        out_shape=[jax.ShapeDtypeStruct(shape, F32), jax.ShapeDtypeStruct((2, *shape[1:]), BF16)],
        compiler_params=pltpu.CompilerParams(vmem_limit_bytes=16 << 20),
        name="total",
    )(*terms)


def finish_kernel(normalizer, pos_ref, own_ref, behind_ref, out):
    member = pos_ref[0]
    for distance in range(ROUNDS):
        result = own_ref[distance]
        if distance >= 2:
            result = jnp.where(distance < member + 2, result, behind_ref[distance - 2].astype(F32))
        out[:, distance, :] = (result * normalizer)[:LAGS]


def finish(pos, own, behind, normalizer):
    return pl.pallas_call(
        functools.partial(finish_kernel, normalizer),
        in_specs=[pl.BlockSpec(memory_space=pltpu.SMEM)] + [pl.BlockSpec(memory_space=pltpu.VMEM)] * 2,
        out_shape=jax.ShapeDtypeStruct((LAGS, ROUNDS, own.shape[2]), F32),
        compiler_params=pltpu.CompilerParams(vmem_limit_bytes=16 << 20),
        name="finish",
    )(pos, own, behind)


def make_tables(channels, freq_total, freq_local):
    half = 3 * channels // 4
    wave = 2 * np.arange(half) + 1
    period = 4 * half
    fwd_angle = 2.0 * np.pi / period * ((wave[:, None] * np.arange(channels)[None, :]) % period)
    fwd = np.concatenate([np.cos(fwd_angle), np.sin(fwd_angle)], axis=0)
    inv_angle = 2.0 * np.pi / period * ((wave[:, None] * (np.arange(channels) - channels // 2)[None, :]) % period)
    inv = np.concatenate([np.cos(inv_angle), -np.sin(inv_angle)], axis=0).T
    rows = -(-LAGS // 16) * 16
    bins = freq_local // (GROUP * PARTS)
    tau = np.arange(LAGS) - (LAGS - 1) // 2
    lag_angle = np.pi / freq_total * ((tau[:, None] * np.arange(freq_total)[None, :]) % (2 * freq_total))
    lag_angle = lag_angle.reshape(LAGS, freq_total // bins, bins).transpose(1, 0, 2)
    lag = np.zeros((freq_total // bins, rows, 2 * LANES), np.float64)
    lag[:, :LAGS, :bins] = np.cos(lag_angle)
    lag[:, :LAGS, LANES : LANES + bins] = -np.sin(lag_angle)
    return tuple(table.astype(ml_dtypes.bfloat16) for table in (fwd, lag, inv))


def on_device(n_frq, spectra, channel_valid):
    _, channels, windows, freq_local = spectra.shape
    n_blk = lax.axis_size("blk")
    freq_total = freq_local * n_frq
    fwd, lag, inv = make_tables(channels, freq_total, freq_local)
    tables = (jnp.asarray(fwd), jnp.asarray(lag), jnp.asarray(inv))
    normalizer = 1.0 / math.sqrt(windows * channels * freq_total) / (3 * channels // 2)
    member = lax.rem(lax.axis_index("blk"), GROUP)
    side = lax.axis_index("frq")
    pos = jnp.stack([member, side]).astype(jnp.int32)
    valid = channel_valid[None, :]
    bins = freq_local // (GROUP * PARTS)
    if bins != LANES:
        split = spectra.reshape(2, channels, windows, GROUP * PARTS, bins)
        split = jnp.pad(split, ((0, 0),) * 4 + ((0, LANES - bins),))
        spectra = split.reshape(2, channels, windows, GROUP * PARTS * LANES)

    def move(value, target):
        pairs = [(i, target(i)) for i in range(n_blk) if 0 <= target(i) < n_blk]
        return lax.ppermute(value, "blk", pairs)

    def swap(value, flip):
        return move(value, lambda i: i ^ flip)

    def up(i):
        return i % GROUP >= 2

    def forward(value):
        return move(value, lambda i: i - GROUP if up(i) else i + GROUP)

    def near(value, flip):
        return move(value, lambda i: (i ^ flip) + (GROUP if up(i) else -GROUP))

    y02, y03, y12, y13, core, core0, core1, own0, own1 = whiten(
        spectra,
        valid,
        [[(2, 0)], [(3, 0)], [(2, 1)], [(3, 1)], [(1, 0), (1, 1)], [(1, 0)], [(1, 1)], [(0, 0)], [(0, 1)]],
    )
    y02_came = swap(y02, 2)
    y03_came = swap(y03, 3)
    core_came = swap(core, 1)
    near00 = near(own0, 0)
    near01 = near(core0, 1)
    y12_came = swap(y12, 2)
    far02 = forward(after(y02_came, core_came))
    near10 = near(after(own1, near00), 0)
    y13_came = swap(after(y13, y02_came), 3)
    far03 = forward(after(y03_came, near00, far02))
    near11 = near(after(core1, near01), 1)
    far12 = forward(after(y12_came, far02))
    far13 = forward(after(y13_came, far03))

    blocks0 = [[(own0, 0)], [(core_came, 0)], [(y02_came, 0)], [(y03_came, 0)], [(near00, 0)], [(near01, 0)], [(far02, 0)], [(far03, 0)]]
    blocks1 = [[(own1, 0)], [(core_came, 1)], [(y12_came, 0)], [(y13_came, 0)], [(near10, 0)], [(near11, 0)], [(far12, 0)], [(far13, 0)]]
    partial = correlate(after(pos, y13_came), 0, blocks0, tables)
    keep, send = correlate(pos, 1, blocks1, tables, partial)
    came = swap(send, 1)

    if n_frq == 2:

        def both(value, flip, cross):
            flat = [(i, x) for i in range(n_blk) for x in range(2)]
            pairs = [(2 * i + x, 2 * (i ^ flip) + (x ^ cross)) for i, x in flat]
            return lax.ppermute(value, ("blk", "frq"), pairs)

        mine, other, far_mine, far_other = halves(pos, keep, came)
        terms = [mine, both(other, 0, 1), both(far_mine, 2, 0), both(far_other, 2, 1)]
    else:
        both = keep.astype(F32) + came.astype(F32)
        both = both[0] + swap(both[1].astype(BF16), 2).astype(F32)
        terms = [lax.psum_scatter(both, "frq", scatter_dimension=2, tiled=True)]
    result, back = total(*terms)
    behind = move(back, lambda i: n_blk if up(i) else i + GROUP)
    stacked = finish(pos, result, behind, normalizer)
    return jnp.transpose(stacked, (1, 0, 2))[None]


def solution(mesh):
    return jax.shard_map(
        functools.partial(on_device, mesh.shape["frq"]),
        mesh=mesh,
        in_specs=(P(None, "blk", None, "frq"), P("blk")),
        out_specs=P("blk", None, None, "frq"),
        check_vma=False,
    )
```

```python
import functools
import math

import jax
import jax.numpy as jnp
import ml_dtypes
import numpy as np
from jax import lax
from jax.experimental import pallas as pl
from jax.experimental.pallas import tpu as pltpu
from jax.sharding import PartitionSpec as P

LAGS = 201
ROUNDS = 4
GROUP = 4
PARTS = 2
LANES = 128
F32, BF16 = jnp.float32, jnp.bfloat16


def after(value, *others):
    return lax.optimization_barrier((value, others))[0]


def pair_list():
    pairs = []
    for own in range(GROUP):
        for distance in range(1, ROUNDS + 1):
            far = own - distance
            if far >= 0:
                pairs.append((own, far))
            elif far + GROUP >= 2:
                pairs.append((own, far + GROUP + 2))
            else:
                pairs.append((own + 6, far + GROUP))
    return pairs


def pieces_of(items):
    return sorted({piece for item in items for piece in item})


def whiten_kernel(items, tile, valid_ref, spectra_ref, *refs):
    outs, (raw, held, ready, load_sem, store_sem) = refs[: len(items)], refs[len(items) :]
    member = lax.rem(lax.axis_index("blk"), GROUP)
    _, channels, windows, freqs = spectra_ref.shape
    parts = freqs // (GROUP * LANES)
    pieces = pieces_of(items)
    steps = channels // tile

    def load(step):
        rows = pl.ds(pl.multiple_of(step * tile, tile), tile)
        return pltpu.make_async_copy(spectra_ref.at[:, rows], raw.at[:, rows], load_sem.at[step])

    def stores(step):
        rows = pl.ds(pl.multiple_of(step * tile, tile), tile)
        copies = []
        for out, item in zip(outs, items):
            for index, piece in enumerate(item):
                source = ready.at[pieces.index(piece), :, rows]
                copies.append(pltpu.make_async_copy(source, out.at[index, :, rows], store_sem.at[step, len(copies)]))
        return copies

    for step in range(steps):
        load(step).start()

    def work(step, carry):
        load(step).wait()
        rows = pl.ds(pl.multiple_of(step * tile, tile), tile)
        place = (tile, channels)
        row = lax.broadcasted_iota(jnp.int32, place, 0) + step * tile
        here = row == lax.broadcasted_iota(jnp.int32, place, 1)
        valid = jnp.sum(jnp.where(here, valid_ref[...].astype(F32), 0.0), axis=1, keepdims=True)
        for at, (flip, part) in enumerate(pieces):
            lanes = pl.ds(pl.multiple_of(((member ^ flip) * parts + part) * LANES, LANES), LANES)
            for half in range(2):
                held[at, half] = raw[half, rows, :, lanes].reshape(tile * windows, LANES).astype(F32)
            values = [
                [held[at, half, pl.ds(w, tile, stride=windows), :] for half in range(2)] for w in range(windows)
            ]
            power = values[0][0] * values[0][0] + values[0][1] * values[0][1]
            for real, imag in values[1:]:
                power = power + (real * real + imag * imag)
            scale = valid * jnp.minimum(lax.rsqrt(power * (1.0 / windows)), 2.0)
            for w in range(windows):
                both = jnp.concatenate([values[w][half] * scale for half in range(2)], axis=1)
                ready[at, w, rows, :] = both.astype(BF16)
        for copy in stores(step):
            copy.start()
        return carry

    lax.fori_loop(0, steps, work, 0)

    def drain(step, carry):
        for copy in stores(step):
            copy.wait()
        return carry

    lax.fori_loop(0, steps, drain, 0)


def whiten(spectra, valid, items):
    _, channels, windows, _ = spectra.shape
    tile = min(32, channels)
    count = len(pieces_of(items))
    anywhere = pl.BlockSpec(memory_space=pl.ANY)
    return pl.pallas_call(
        functools.partial(whiten_kernel, items, tile),
        in_specs=[pl.BlockSpec(memory_space=pltpu.VMEM), anywhere],
        out_specs=[anywhere] * len(items),
        scratch_shapes=[
            pltpu.VMEM(spectra.shape, BF16),
            pltpu.VMEM((count, 2, tile * windows, LANES), F32),
            pltpu.VMEM((count, windows, channels, 2 * LANES), BF16),
            pltpu.SemaphoreType.DMA((channels // tile,)),
            pltpu.SemaphoreType.DMA((channels // tile, sum(len(item) for item in items))),
        ],
        out_shape=[jax.ShapeDtypeStruct((len(item), windows, channels, 2 * LANES), BF16) for item in items],
        compiler_params=pltpu.CompilerParams(vmem_limit_bytes=56 << 20),
        cost_estimate=pl.CostEstimate(flops=0, bytes_accessed=1000, transcendentals=0),
        name="whiten",
    )(valid, spectra)


def correlate_kernel(pairs, places, part, pos_ref, *refs):
    count, pieces = 2 * GROUP, sum(len(block) for block in places)
    blocks, before = iter(refs[:pieces]), refs[pieces:-16]
    fwd_in, lag_in, inv_in, keep_out, send_out = refs[-16:-11]
    held, held_before, fwd_ref, lag_ref, inv_ref, hat, plus, cross, turned, result, sem = refs[-11:]
    member = pos_ref[0]
    half = fwd_ref.shape[0] // 2
    windows = held.shape[1]

    def load(index, source, target):
        copy = pltpu.make_async_copy(source, target, sem.at[index])
        copy.start()
        return copy

    fwd_load = load(pieces, fwd_in, fwd_ref)
    loads = []
    for index, block in enumerate(places):
        first = 0
        for place in block:
            source = next(blocks).at[place]
            target = held.at[index, pl.ds(first, source.shape[0])]
            loads.append((index, load(len(loads), source, target)))
            first += source.shape[0]
    later = [
        load(pieces + 1, inv_in, inv_ref),
        load(pieces + 2, lag_in.at[(pos_ref[1] * GROUP + member) * PARTS + part], lag_ref),
    ]
    later += [load(pieces + 3 + index, source, held_before.at[index]) for index, source in enumerate(before)]
    fwd_load.wait()
    for index in range(count):
        slot = member ^ (index % GROUP)
        if index >= GROUP:
            slot = jnp.where(slot < 2, slot + 6, slot + 2)
        for target, copy in loads:
            if target == index:
                copy.wait()
        for w in range(windows):
            terms = jnp.dot(fwd_ref[...], held[index, w], preferred_element_type=F32)
            cos_r, cos_i = terms[:half, :LANES], terms[:half, LANES:]
            sin_r, sin_i = terms[half:, :LANES], terms[half:, LANES:]
            hat[slot, w, 0] = cos_r + sin_i
            hat[slot, w, 1] = cos_i - sin_r
            hat[slot, w, 2] = cos_r - sin_i
            hat[slot, w, 3] = cos_i + sin_r

    def products(step, carry):
        rows = pl.ds(pl.multiple_of(step * 8, 8), 8)
        odd_rows = pl.ds(pl.multiple_of(half + step * 8, 8), 8)
        for sign in range(2):
            sums = [None] * (2 * len(pairs))
            for win in range(windows):
                real = [hat[slot, win, 2 * sign, rows, :] for slot in range(count)]
                imag = [hat[slot, win, 2 * sign + 1, rows, :] for slot in range(count)]
                for n, (own, far) in enumerate(pairs):
                    part_r = real[own] * real[far] + imag[own] * imag[far]
                    part_i = imag[own] * real[far] - real[own] * imag[far]
                    sums[2 * n] = part_r if win == 0 else sums[2 * n] + part_r
                    sums[2 * n + 1] = part_i if win == 0 else sums[2 * n + 1] + part_i
            for n in range(len(pairs)):
                if sign == 0:
                    plus[2 * n], plus[2 * n + 1] = sums[2 * n], sums[2 * n + 1]
                else:
                    plus_r, plus_i = plus[2 * n], plus[2 * n + 1]
                    minus_r, minus_i = sums[2 * n], sums[2 * n + 1]
                    cross[n, rows, :LANES] = plus_r + minus_r
                    cross[n, rows, LANES:] = plus_i + minus_i
                    cross[n, odd_rows, :LANES] = plus_i - minus_i
                    cross[n, odd_rows, LANES:] = minus_r - plus_r
        return carry

    lax.fori_loop(0, half // 8, products, 0)
    for copy in later:
        copy.wait()

    def turn(n, carry):
        turned[n] = jnp.dot(inv_ref[...], cross[n].astype(BF16), preferred_element_type=F32).astype(BF16)
        return carry

    lax.fori_loop(0, len(pairs), turn, 0, unroll=8)
    stores = []
    for flip in (1, 3, 0, 2):
        for distance in range(ROUNDS):
            n = (member ^ flip) * ROUNDS + distance
            total = lax.dot_general(lag_ref[...], turned[n], (((1,), (1,)), ((), ())), preferred_element_type=F32)
            if before:
                total = total + held_before[flip % 2, flip // 2, distance].astype(F32)
            result[flip, distance] = total.astype(BF16)
        out = (keep_out, send_out)[flip % 2].at[flip // 2]
        stores.append(pltpu.make_async_copy(result.at[flip], out, sem.at[pieces + 5 + flip]))
        stores[-1].start()
    for copy in stores:
        copy.wait()


def correlate(pos, part, blocks, tables, before=()):
    fwd, lag, inv = tables
    windows = sum(array.shape[1] for array, _ in blocks[0])
    channels, lanes = blocks[0][0][0].shape[2:]
    rows = lag.shape[1]
    pairs = pair_list()
    half = fwd.shape[0] // 2
    places = [[place for _, place in block] for block in blocks]
    arrays = [array for block in blocks for array, _ in block]
    shape = (2, ROUNDS, rows, channels)
    anywhere = pl.BlockSpec(memory_space=pl.ANY)
    return pl.pallas_call(
        functools.partial(correlate_kernel, pairs, places, part),
        in_specs=[pl.BlockSpec(memory_space=pltpu.SMEM)] + [anywhere] * (len(arrays) + len(before) + 3),
        out_specs=[anywhere, anywhere],
        scratch_shapes=[
            pltpu.VMEM((2 * GROUP, windows, channels, lanes), BF16),
            pltpu.VMEM((2, *shape), BF16),
            pltpu.VMEM(fwd.shape, BF16),
            pltpu.VMEM(lag.shape[1:], BF16),
            pltpu.VMEM(inv.shape, BF16),
            pltpu.VMEM((2 * GROUP, windows, 4, half, LANES), F32),
            pltpu.VMEM((2 * len(pairs), 8, LANES), F32),
            pltpu.VMEM((len(pairs), 2 * half, 2 * LANES), F32),
            pltpu.VMEM((len(pairs), channels, 2 * LANES), BF16),
            pltpu.VMEM((GROUP, *shape[1:]), BF16),
            pltpu.SemaphoreType.DMA((len(arrays) + 9,)),
        ],
        out_shape=[jax.ShapeDtypeStruct(shape, BF16)] * 2,
        compiler_params=pltpu.CompilerParams(vmem_limit_bytes=62 << 20),
        cost_estimate=pl.CostEstimate(flops=0, bytes_accessed=1000, transcendentals=0),
        name="correlate",
    )(pos, *arrays, *before, fwd, lag, inv)


def halves_kernel(pos_ref, *refs):
    for index in range(4):
        keep, came, out = refs[index], refs[4 + index], refs[8 + index]
        out[...] = (keep[0].astype(F32) + came[0].astype(F32)).astype(out.dtype)


def halves(pos, keep, came):
    _, rounds, rows, channels = keep.shape
    width = channels // 2
    specs = [
        pl.BlockSpec((1, rounds, rows, width), lambda i, pos, f=f, g=g: (f, 0, 0, pos[1] ^ g))
        for f in range(2)
        for g in range(2)
    ]
    out_spec = pl.BlockSpec((rounds, rows, width), lambda i, pos: (0, 0, 0))
    return pl.pallas_call(
        halves_kernel,
        grid_spec=pltpu.PrefetchScalarGridSpec(
            num_scalar_prefetch=1, grid=(1,), in_specs=specs * 2, out_specs=[out_spec] * 4
        ),
        out_shape=[jax.ShapeDtypeStruct((rounds, rows, width), t) for t in (F32, BF16, BF16, BF16)],
        compiler_params=pltpu.CompilerParams(vmem_limit_bytes=16 << 20),
        name="halves",
    )(pos, *([keep] * 4), *([came] * 4))


def total_kernel(*refs):
    *terms, out, back = refs
    for distance in range(ROUNDS):
        result = terms[0][distance].astype(F32)
        for term in terms[1:]:
            result = result + term[distance].astype(F32)
        out[distance] = result
        if distance >= 2:
            back[distance - 2] = result.astype(BF16)


def total(*terms):
    shape = terms[0].shape
    return pl.pallas_call(
        total_kernel,
        out_shape=[jax.ShapeDtypeStruct(shape, F32), jax.ShapeDtypeStruct((2, *shape[1:]), BF16)],
        compiler_params=pltpu.CompilerParams(vmem_limit_bytes=16 << 20),
        name="total",
    )(*terms)


def finish_kernel(normalizer, pos_ref, own_ref, behind_ref, out):
    member = pos_ref[0]
    for distance in range(ROUNDS):
        result = own_ref[distance]
        if distance >= 2:
            result = jnp.where(distance < member + 2, result, behind_ref[distance - 2].astype(F32))
        out[:, distance, :] = (result * normalizer)[:LAGS]


def finish(pos, own, behind, normalizer):
    return pl.pallas_call(
        functools.partial(finish_kernel, normalizer),
        in_specs=[pl.BlockSpec(memory_space=pltpu.SMEM)] + [pl.BlockSpec(memory_space=pltpu.VMEM)] * 2,
        out_shape=jax.ShapeDtypeStruct((LAGS, ROUNDS, own.shape[2]), F32),
        compiler_params=pltpu.CompilerParams(vmem_limit_bytes=16 << 20),
        name="finish",
    )(pos, own, behind)


def make_tables(channels, freq_total, freq_local):
    half = 3 * channels // 4
    wave = 2 * np.arange(half) + 1
    period = 4 * half
    fwd_angle = 2.0 * np.pi / period * ((wave[:, None] * np.arange(channels)[None, :]) % period)
    fwd = np.concatenate([np.cos(fwd_angle), np.sin(fwd_angle)], axis=0)
    inv_angle = 2.0 * np.pi / period * ((wave[:, None] * (np.arange(channels) - channels // 2)[None, :]) % period)
    inv = np.concatenate([np.cos(inv_angle), -np.sin(inv_angle)], axis=0).T
    rows = -(-LAGS // 16) * 16
    bins = freq_local // (GROUP * PARTS)
    tau = np.arange(LAGS) - (LAGS - 1) // 2
    lag_angle = np.pi / freq_total * ((tau[:, None] * np.arange(freq_total)[None, :]) % (2 * freq_total))
    lag_angle = lag_angle.reshape(LAGS, freq_total // bins, bins).transpose(1, 0, 2)
    lag = np.zeros((freq_total // bins, rows, 2 * LANES), np.float64)
    lag[:, :LAGS, :bins] = np.cos(lag_angle)
    lag[:, :LAGS, LANES : LANES + bins] = -np.sin(lag_angle)
    return tuple(table.astype(ml_dtypes.bfloat16) for table in (fwd, lag, inv))


def on_device(n_frq, spectra, channel_valid):
    _, channels, windows, freq_local = spectra.shape
    n_blk = lax.axis_size("blk")
    freq_total = freq_local * n_frq
    fwd, lag, inv = make_tables(channels, freq_total, freq_local)
    tables = (jnp.asarray(fwd), jnp.asarray(lag), jnp.asarray(inv))
    normalizer = 1.0 / math.sqrt(windows * channels * freq_total) / (3 * channels // 2)
    member = lax.rem(lax.axis_index("blk"), GROUP)
    side = lax.axis_index("frq")
    pos = jnp.stack([member, side]).astype(jnp.int32)
    valid = channel_valid[None, :]
    bins = freq_local // (GROUP * PARTS)
    if bins != LANES:
        split = spectra.reshape(2, channels, windows, GROUP * PARTS, bins)
        split = jnp.pad(split, ((0, 0),) * 4 + ((0, LANES - bins),))
        spectra = split.reshape(2, channels, windows, GROUP * PARTS * LANES)

    def move(value, target):
        pairs = [(i, target(i)) for i in range(n_blk) if 0 <= target(i) < n_blk]
        return lax.ppermute(value, "blk", pairs)

    def swap(value, flip):
        return move(value, lambda i: i ^ flip)

    def up(i):
        return i % GROUP >= 2

    def forward(value):
        return move(value, lambda i: i - GROUP if up(i) else i + GROUP)

    def near(value, flip):
        return move(value, lambda i: (i ^ flip) + (GROUP if up(i) else -GROUP))

    y02, y03, y12, y13, core, core0, core1, own0, own1 = whiten(
        spectra,
        valid,
        [[(2, 0)], [(3, 0)], [(2, 1)], [(3, 1)], [(1, 0), (1, 1)], [(1, 0)], [(1, 1)], [(0, 0)], [(0, 1)]],
    )
    y02_came = swap(y02, 2)
    y03_came = swap(y03, 3)
    core_came = swap(core, 1)
    near00 = near(own0, 0)
    near01 = near(core0, 1)
    y12_came = swap(y12, 2)
    far02 = forward(after(y02_came, core_came))
    near10 = near(after(own1, near00), 0)
    y13_came = swap(after(y13, y02_came), 3)
    far03 = forward(after(y03_came, near00, far02))
    near11 = near(after(core1, near01), 1)
    far12 = forward(after(y12_came, far02))
    far13 = forward(after(y13_came, far03))

    blocks0 = [[(own0, 0)], [(core_came, 0)], [(y02_came, 0)], [(y03_came, 0)], [(near00, 0)], [(near01, 0)], [(far02, 0)], [(far03, 0)]]
    blocks1 = [[(own1, 0)], [(core_came, 1)], [(y12_came, 0)], [(y13_came, 0)], [(near10, 0)], [(near11, 0)], [(far12, 0)], [(far13, 0)]]
    partial = correlate(after(pos, y13_came), 0, blocks0, tables)
    keep, send = correlate(pos, 1, blocks1, tables, partial)
    came = swap(send, 1)

    if n_frq == 2:

        def both(value, flip, cross):
            flat = [(i, x) for i in range(n_blk) for x in range(2)]
            pairs = [(2 * i + x, 2 * (i ^ flip) + (x ^ cross)) for i, x in flat]
            return lax.ppermute(value, ("blk", "frq"), pairs)

        mine, other, far_mine, far_other = halves(pos, keep, came)
        terms = [mine, both(other, 0, 1), both(far_mine, 2, 0), both(far_other, 2, 1)]
    else:
        both = keep.astype(F32) + came.astype(F32)
        both = both[0] + swap(both[1].astype(BF16), 2).astype(F32)
        terms = [lax.psum_scatter(both, "frq", scatter_dimension=2, tiled=True)]
    result, back = total(*terms)
    behind = move(back, lambda i: n_blk if up(i) else i + GROUP)
    stacked = finish(pos, result, behind, normalizer)
    return jnp.transpose(stacked, (1, 0, 2))[None]


def solution(mesh):
    return jax.shard_map(
        functools.partial(on_device, mesh.shape["frq"]),
        mesh=mesh,
        in_specs=(P(None, "blk", None, "frq"), P("blk")),
        out_specs=P("blk", None, None, "frq"),
        check_vma=False,
    )
```

```python
import functools
import math

import jax
import jax.numpy as jnp
import ml_dtypes
import numpy as np
from jax import lax
from jax.experimental import pallas as pl
from jax.experimental.pallas import tpu as pltpu
from jax.sharding import PartitionSpec as P

LAGS = 201
ROUNDS = 4
GROUP = 4
PARTS = 2
LANES = 128
F32, BF16 = jnp.float32, jnp.bfloat16


def after(value, *others):
    return lax.optimization_barrier((value, others))[0]


def pair_list():
    pairs = []
    for own in range(GROUP):
        for distance in range(1, ROUNDS + 1):
            far = own - distance
            if far >= 0:
                pairs.append((own, far))
            elif far + GROUP >= 2:
                pairs.append((own, far + GROUP + 2))
            else:
                pairs.append((own + 6, far + GROUP))
    return pairs


def pieces_of(items):
    return sorted({piece for item in items for piece in item})


def whiten_kernel(items, tile, valid_ref, spectra_ref, *refs):
    outs, (raw, held, ready, load_sem, store_sem) = refs[: len(items)], refs[len(items) :]
    member = lax.rem(lax.axis_index("blk"), GROUP)
    _, channels, windows, freqs = spectra_ref.shape
    parts = freqs // (GROUP * LANES)
    pieces = pieces_of(items)
    steps = channels // tile

    def load(step):
        rows = pl.ds(pl.multiple_of(step * tile, tile), tile)
        return pltpu.make_async_copy(spectra_ref.at[:, rows], raw.at[:, rows], load_sem.at[step])

    def stores(step):
        rows = pl.ds(pl.multiple_of(step * tile, tile), tile)
        copies = []
        for out, item in zip(outs, items):
            for index, piece in enumerate(item):
                source = ready.at[pieces.index(piece), :, rows]
                copies.append(pltpu.make_async_copy(source, out.at[index, :, rows], store_sem.at[step, len(copies)]))
        return copies

    for step in range(steps):
        load(step).start()

    def work(step, carry):
        load(step).wait()
        rows = pl.ds(pl.multiple_of(step * tile, tile), tile)
        place = (tile, channels)
        row = lax.broadcasted_iota(jnp.int32, place, 0) + step * tile
        here = row == lax.broadcasted_iota(jnp.int32, place, 1)
        valid = jnp.sum(jnp.where(here, valid_ref[...].astype(F32), 0.0), axis=1, keepdims=True)
        for at, (flip, part) in enumerate(pieces):
            lanes = pl.ds(pl.multiple_of(((member ^ flip) * parts + part) * LANES, LANES), LANES)
            for half in range(2):
                held[at, half] = raw[half, rows, :, lanes].reshape(tile * windows, LANES).astype(F32)
            values = [
                [held[at, half, pl.ds(w, tile, stride=windows), :] for half in range(2)] for w in range(windows)
            ]
            power = values[0][0] * values[0][0] + values[0][1] * values[0][1]
            for real, imag in values[1:]:
                power = power + (real * real + imag * imag)
            scale = valid * jnp.minimum(lax.rsqrt(power * (1.0 / windows)), 2.0)
            for w in range(windows):
                both = jnp.concatenate([values[w][half] * scale for half in range(2)], axis=1)
                ready[at, w, rows, :] = both.astype(BF16)
        for copy in stores(step):
            copy.start()
        return carry

    lax.fori_loop(0, steps, work, 0)

    def drain(step, carry):
        for copy in stores(step):
            copy.wait()
        return carry

    lax.fori_loop(0, steps, drain, 0)


def whiten(spectra, valid, items):
    _, channels, windows, _ = spectra.shape
    tile = min(64, channels)
    count = len(pieces_of(items))
    anywhere = pl.BlockSpec(memory_space=pl.ANY)
    return pl.pallas_call(
        functools.partial(whiten_kernel, items, tile),
        in_specs=[pl.BlockSpec(memory_space=pltpu.VMEM), anywhere],
        out_specs=[anywhere] * len(items),
        scratch_shapes=[
            pltpu.VMEM(spectra.shape, BF16),
            pltpu.VMEM((count, 2, tile * windows, LANES), F32),
            pltpu.VMEM((count, windows, channels, 2 * LANES), BF16),
            pltpu.SemaphoreType.DMA((channels // tile,)),
            pltpu.SemaphoreType.DMA((channels // tile, sum(len(item) for item in items))),
        ],
        out_shape=[jax.ShapeDtypeStruct((len(item), windows, channels, 2 * LANES), BF16) for item in items],
        compiler_params=pltpu.CompilerParams(vmem_limit_bytes=56 << 20),
        cost_estimate=pl.CostEstimate(flops=0, bytes_accessed=1000, transcendentals=0),
        name="whiten",
    )(valid, spectra)


def correlate_kernel(pairs, places, part, pos_ref, *refs):
    count, pieces = 2 * GROUP, sum(len(block) for block in places)
    blocks, before = iter(refs[:pieces]), refs[pieces:-16]
    fwd_in, lag_in, inv_in, keep_out, send_out = refs[-16:-11]
    held, held_before, fwd_ref, lag_ref, inv_ref, hat, plus, cross, turned, result, sem = refs[-11:]
    member = pos_ref[0]
    half = fwd_ref.shape[0] // 2
    windows = held.shape[1]

    def load(index, source, target):
        copy = pltpu.make_async_copy(source, target, sem.at[index])
        copy.start()
        return copy

    fwd_load = load(pieces, fwd_in, fwd_ref)
    loads = []
    for index, block in enumerate(places):
        first = 0
        for place in block:
            source = next(blocks).at[place]
            target = held.at[index, pl.ds(first, source.shape[0])]
            loads.append((index, load(len(loads), source, target)))
            first += source.shape[0]
    later = [
        load(pieces + 1, inv_in, inv_ref),
        load(pieces + 2, lag_in.at[(pos_ref[1] * GROUP + member) * PARTS + part], lag_ref),
    ]
    later += [load(pieces + 3 + index, source, held_before.at[index]) for index, source in enumerate(before)]
    fwd_load.wait()
    for index in range(count):
        slot = member ^ (index % GROUP)
        if index >= GROUP:
            slot = jnp.where(slot < 2, slot + 6, slot + 2)
        for target, copy in loads:
            if target == index:
                copy.wait()
        for w in range(windows):
            terms = jnp.dot(fwd_ref[...], held[index, w], preferred_element_type=F32)
            cos_r, cos_i = terms[:half, :LANES], terms[:half, LANES:]
            sin_r, sin_i = terms[half:, :LANES], terms[half:, LANES:]
            hat[slot, w, 0] = cos_r + sin_i
            hat[slot, w, 1] = cos_i - sin_r
            hat[slot, w, 2] = cos_r - sin_i
            hat[slot, w, 3] = cos_i + sin_r

    def products(step, carry):
        rows = pl.ds(pl.multiple_of(step * 8, 8), 8)
        odd_rows = pl.ds(pl.multiple_of(half + step * 8, 8), 8)
        for sign in range(2):
            sums = [None] * (2 * len(pairs))
            for win in range(windows):
                real = [hat[slot, win, 2 * sign, rows, :] for slot in range(count)]
                imag = [hat[slot, win, 2 * sign + 1, rows, :] for slot in range(count)]
                for n, (own, far) in enumerate(pairs):
                    part_r = real[own] * real[far] + imag[own] * imag[far]
                    part_i = imag[own] * real[far] - real[own] * imag[far]
                    sums[2 * n] = part_r if win == 0 else sums[2 * n] + part_r
                    sums[2 * n + 1] = part_i if win == 0 else sums[2 * n + 1] + part_i
            for n in range(len(pairs)):
                if sign == 0:
                    plus[2 * n], plus[2 * n + 1] = sums[2 * n], sums[2 * n + 1]
                else:
                    plus_r, plus_i = plus[2 * n], plus[2 * n + 1]
                    minus_r, minus_i = sums[2 * n], sums[2 * n + 1]
                    cross[n, rows, :LANES] = plus_r + minus_r
                    cross[n, rows, LANES:] = plus_i + minus_i
                    cross[n, odd_rows, :LANES] = plus_i - minus_i
                    cross[n, odd_rows, LANES:] = minus_r - plus_r
        return carry

    lax.fori_loop(0, half // 8, products, 0)
    for copy in later:
        copy.wait()

    def turn(n, carry):
        turned[n] = jnp.dot(inv_ref[...], cross[n].astype(BF16), preferred_element_type=F32).astype(BF16)
        return carry

    lax.fori_loop(0, len(pairs), turn, 0, unroll=8)
    stores = []
    for flip in (1, 3, 0, 2):
        for distance in range(ROUNDS):
            n = (member ^ flip) * ROUNDS + distance
            total = lax.dot_general(lag_ref[...], turned[n], (((1,), (1,)), ((), ())), preferred_element_type=F32)
            if before:
                total = total + held_before[flip % 2, flip // 2, distance].astype(F32)
            result[flip, distance] = total.astype(BF16)
        out = (keep_out, send_out)[flip % 2].at[flip // 2]
        stores.append(pltpu.make_async_copy(result.at[flip], out, sem.at[pieces + 5 + flip]))
        stores[-1].start()
    for copy in stores:
        copy.wait()


def correlate(pos, part, blocks, tables, before=()):
    fwd, lag, inv = tables
    windows = sum(array.shape[1] for array, _ in blocks[0])
    channels, lanes = blocks[0][0][0].shape[2:]
    rows = lag.shape[1]
    pairs = pair_list()
    half = fwd.shape[0] // 2
    places = [[place for _, place in block] for block in blocks]
    arrays = [array for block in blocks for array, _ in block]
    shape = (2, ROUNDS, rows, channels)
    anywhere = pl.BlockSpec(memory_space=pl.ANY)
    return pl.pallas_call(
        functools.partial(correlate_kernel, pairs, places, part),
        in_specs=[pl.BlockSpec(memory_space=pltpu.SMEM)] + [anywhere] * (len(arrays) + len(before) + 3),
        out_specs=[anywhere, anywhere],
        scratch_shapes=[
            pltpu.VMEM((2 * GROUP, windows, channels, lanes), BF16),
            pltpu.VMEM((2, *shape), BF16),
            pltpu.VMEM(fwd.shape, BF16),
            pltpu.VMEM(lag.shape[1:], BF16),
            pltpu.VMEM(inv.shape, BF16),
            pltpu.VMEM((2 * GROUP, windows, 4, half, LANES), F32),
            pltpu.VMEM((2 * len(pairs), 8, LANES), F32),
            pltpu.VMEM((len(pairs), 2 * half, 2 * LANES), F32),
            pltpu.VMEM((len(pairs), channels, 2 * LANES), BF16),
            pltpu.VMEM((GROUP, *shape[1:]), BF16),
            pltpu.SemaphoreType.DMA((len(arrays) + 9,)),
        ],
        out_shape=[jax.ShapeDtypeStruct(shape, BF16)] * 2,
        compiler_params=pltpu.CompilerParams(vmem_limit_bytes=62 << 20),
        cost_estimate=pl.CostEstimate(flops=0, bytes_accessed=1000, transcendentals=0),
        name="correlate",
    )(pos, *arrays, *before, fwd, lag, inv)


def halves_kernel(pos_ref, *refs):
    for index in range(4):
        keep, came, out = refs[index], refs[4 + index], refs[8 + index]
        out[...] = (keep[0].astype(F32) + came[0].astype(F32)).astype(out.dtype)


def halves(pos, keep, came):
    _, rounds, rows, channels = keep.shape
    width = channels // 2
    specs = [
        pl.BlockSpec((1, rounds, rows, width), lambda i, pos, f=f, g=g: (f, 0, 0, pos[1] ^ g))
        for f in range(2)
        for g in range(2)
    ]
    out_spec = pl.BlockSpec((rounds, rows, width), lambda i, pos: (0, 0, 0))
    return pl.pallas_call(
        halves_kernel,
        grid_spec=pltpu.PrefetchScalarGridSpec(
            num_scalar_prefetch=1, grid=(1,), in_specs=specs * 2, out_specs=[out_spec] * 4
        ),
        out_shape=[jax.ShapeDtypeStruct((rounds, rows, width), t) for t in (F32, BF16, BF16, BF16)],
        compiler_params=pltpu.CompilerParams(vmem_limit_bytes=16 << 20),
        name="halves",
    )(pos, *([keep] * 4), *([came] * 4))


def total_kernel(*refs):
    *terms, out, back = refs
    for distance in range(ROUNDS):
        result = terms[0][distance].astype(F32)
        for term in terms[1:]:
            result = result + term[distance].astype(F32)
        out[distance] = result
        if distance >= 2:
            back[distance - 2] = result.astype(BF16)


def total(*terms):
    shape = terms[0].shape
    return pl.pallas_call(
        total_kernel,
        out_shape=[jax.ShapeDtypeStruct(shape, F32), jax.ShapeDtypeStruct((2, *shape[1:]), BF16)],
        compiler_params=pltpu.CompilerParams(vmem_limit_bytes=16 << 20),
        name="total",
    )(*terms)


def finish_kernel(normalizer, pos_ref, own_ref, behind_ref, out):
    member = pos_ref[0]
    for distance in range(ROUNDS):
        result = own_ref[distance]
        if distance >= 2:
            result = jnp.where(distance < member + 2, result, behind_ref[distance - 2].astype(F32))
        out[:, distance, :] = (result * normalizer)[:LAGS]


def finish(pos, own, behind, normalizer):
    return pl.pallas_call(
        functools.partial(finish_kernel, normalizer),
        in_specs=[pl.BlockSpec(memory_space=pltpu.SMEM)] + [pl.BlockSpec(memory_space=pltpu.VMEM)] * 2,
        out_shape=jax.ShapeDtypeStruct((LAGS, ROUNDS, own.shape[2]), F32),
        compiler_params=pltpu.CompilerParams(vmem_limit_bytes=16 << 20),
        name="finish",
    )(pos, own, behind)


def make_tables(channels, freq_total, freq_local):
    half = 3 * channels // 4
    wave = 2 * np.arange(half) + 1
    period = 4 * half
    fwd_angle = 2.0 * np.pi / period * ((wave[:, None] * np.arange(channels)[None, :]) % period)
    fwd = np.concatenate([np.cos(fwd_angle), np.sin(fwd_angle)], axis=0)
    inv_angle = 2.0 * np.pi / period * ((wave[:, None] * (np.arange(channels) - channels // 2)[None, :]) % period)
    inv = np.concatenate([np.cos(inv_angle), -np.sin(inv_angle)], axis=0).T
    rows = -(-LAGS // 16) * 16
    bins = freq_local // (GROUP * PARTS)
    tau = np.arange(LAGS) - (LAGS - 1) // 2
    lag_angle = np.pi / freq_total * ((tau[:, None] * np.arange(freq_total)[None, :]) % (2 * freq_total))
    lag_angle = lag_angle.reshape(LAGS, freq_total // bins, bins).transpose(1, 0, 2)
    lag = np.zeros((freq_total // bins, rows, 2 * LANES), np.float64)
    lag[:, :LAGS, :bins] = np.cos(lag_angle)
    lag[:, :LAGS, LANES : LANES + bins] = -np.sin(lag_angle)
    return tuple(table.astype(ml_dtypes.bfloat16) for table in (fwd, lag, inv))


def on_device(n_frq, spectra, channel_valid):
    _, channels, windows, freq_local = spectra.shape
    n_blk = lax.axis_size("blk")
    freq_total = freq_local * n_frq
    fwd, lag, inv = make_tables(channels, freq_total, freq_local)
    tables = (jnp.asarray(fwd), jnp.asarray(lag), jnp.asarray(inv))
    normalizer = 1.0 / math.sqrt(windows * channels * freq_total) / (3 * channels // 2)
    member = lax.rem(lax.axis_index("blk"), GROUP)
    side = lax.axis_index("frq")
    pos = jnp.stack([member, side]).astype(jnp.int32)
    valid = channel_valid[None, :]
    bins = freq_local // (GROUP * PARTS)
    if bins != LANES:
        split = spectra.reshape(2, channels, windows, GROUP * PARTS, bins)
        split = jnp.pad(split, ((0, 0),) * 4 + ((0, LANES - bins),))
        spectra = split.reshape(2, channels, windows, GROUP * PARTS * LANES)

    def move(value, target):
        pairs = [(i, target(i)) for i in range(n_blk) if 0 <= target(i) < n_blk]
        return lax.ppermute(value, "blk", pairs)

    def swap(value, flip):
        return move(value, lambda i: i ^ flip)

    def up(i):
        return i % GROUP >= 2

    def forward(value):
        return move(value, lambda i: i - GROUP if up(i) else i + GROUP)

    def near(value, flip):
        return move(value, lambda i: (i ^ flip) + (GROUP if up(i) else -GROUP))

    y02, y03, y12, y13, core, core0, core1, own0, own1 = whiten(
        spectra,
        valid,
        [[(2, 0)], [(3, 0)], [(2, 1)], [(3, 1)], [(1, 0), (1, 1)], [(1, 0)], [(1, 1)], [(0, 0)], [(0, 1)]],
    )
    y02_came = swap(y02, 2)
    y03_came = swap(y03, 3)
    core_came = swap(core, 1)
    near00 = near(own0, 0)
    near01 = near(core0, 1)
    y12_came = swap(y12, 2)
    far02 = forward(after(y02_came, core_came))
    near10 = near(after(own1, near00), 0)
    y13_came = swap(after(y13, y02_came), 3)
    far03 = forward(after(y03_came, near00, far02))
    near11 = near(after(core1, near01), 1)
    far12 = forward(after(y12_came, far02))
    far13 = forward(after(y13_came, far03))

    blocks0 = [[(own0, 0)], [(core_came, 0)], [(y02_came, 0)], [(y03_came, 0)], [(near00, 0)], [(near01, 0)], [(far02, 0)], [(far03, 0)]]
    blocks1 = [[(own1, 0)], [(core_came, 1)], [(y12_came, 0)], [(y13_came, 0)], [(near10, 0)], [(near11, 0)], [(far12, 0)], [(far13, 0)]]
    partial = correlate(after(pos, y13_came), 0, blocks0, tables)
    keep, send = correlate(pos, 1, blocks1, tables, partial)
    came = swap(send, 1)

    if n_frq == 2:

        def both(value, flip, cross):
            flat = [(i, x) for i in range(n_blk) for x in range(2)]
            pairs = [(2 * i + x, 2 * (i ^ flip) + (x ^ cross)) for i, x in flat]
            return lax.ppermute(value, ("blk", "frq"), pairs)

        mine, other, far_mine, far_other = halves(pos, keep, came)
        terms = [mine, both(other, 0, 1), both(far_mine, 2, 0), both(far_other, 2, 1)]
    else:
        both = keep.astype(F32) + came.astype(F32)
        both = both[0] + swap(both[1].astype(BF16), 2).astype(F32)
        terms = [lax.psum_scatter(both, "frq", scatter_dimension=2, tiled=True)]
    result, back = total(*terms)
    behind = move(back, lambda i: n_blk if up(i) else i + GROUP)
    stacked = finish(pos, result, behind, normalizer)
    return jnp.transpose(stacked, (1, 0, 2))[None]


def solution(mesh):
    return jax.shard_map(
        functools.partial(on_device, mesh.shape["frq"]),
        mesh=mesh,
        in_specs=(P(None, "blk", None, "frq"), P("blk")),
        out_specs=P("blk", None, None, "frq"),
        check_vma=False,
    )
```
